32 devices in a mesh: head: 2 (over x), blk: 16 (over z, y, core).
Axes of the slice: x: 2, y: 2, z: 4, core: 2. Of those that a mesh axis runs over, the one named last changes fastest.
Arguments:
- queries: bfloat16 [2, 6144, 5120], P('head', 'blk'), may hold values from -8 to 8
- keys: bfloat16 [2, 6144, 5120], P('head', 'blk'), may hold values from -8 to 8
- values: bfloat16 [2, 6144, 5120], P('head', 'blk'), may hold values from -6 to 6
- q_gain: float32 [5120], replicated, may hold values from 0.1 to 1.9
- k_gain: float32 [5120], replicated, may hold values from 0.1 to 1.9
- slopes: float32 [40], P('head'), may hold values from 0.25 to 4
- out_weight: bfloat16 [5120, 5120], P('head', 'blk'), may hold values from -1 to 1
- kv_tiles: int32 [32, 4], replicated, may hold values from 0 to 31, as said below
- tile_frame: int32 [32], replicated, may hold values from 0 to 3, never falling along the last dimension, each value on 1 to 16 neighbouring positions
Outputs:
- mixed: bfloat16 [2, 6144, 5120], P('head', 'blk')
The draws below stay inside these ranges and needn't reach their ends.
Inputs may be any that keep to these rules, and one draw needn't show every extreme that they name: kv_tiles[t, 0] = t; the other entries of row t are distinct tiles other than t, each within 3 tiles of t. `tile_frame`: never falls from one tile to the next.
All inputs are finite; a program needn't handle non-finite values.
Results may differ from the reference program's by a relative error of at most 0.013.
Values may be sent and summed in bfloat16 or wider, within the bound.
A program may use at most 256 MiB of HBM per device.

```python
import math
import jax
import jax.numpy as jnp
import numpy as np
from jax import lax

D = 5120
HEADS = 40
HDIM = 128
TILE = 384
HD = 5120
GROUPS = 2
T_DEV = 384
NTILES = 32
TOKENS = 12288
REACH = 3
WIN = 4
FRAMES = 4
N_HEAD = 2
N_BLK = 16


def paired_rows(key):
    rows = TOKENS // GROUPS
    first = jax.random.fold_in(key, 101)
    second = jax.random.fold_in(key, 102)
    third = jax.random.fold_in(key, 103)
    raw = jax.random.normal(first, (2, GROUPS, rows, HD), jnp.float32)
    column_scale = jnp.exp(jax.random.uniform(second, (2, 1, 1, HD), jnp.float32, math.log(0.3), math.log(3.0)))
    row_scale = jnp.exp(jax.random.uniform(third, (2, GROUPS, rows, 1), jnp.float32, math.log(0.3), math.log(3.0)))
    both = raw * column_scale * row_scale
    query_rows = both[0]
    key_rows = both[1]
    return (jnp.clip(query_rows, -8.0, 8.0), jnp.clip(key_rows, -8.0, 8.0))


def draw_queries(key, part):
    return paired_rows(key)[0].astype(jnp.bfloat16)


def draw_keys(key, part):
    return paired_rows(key)[1].astype(jnp.bfloat16)


def draw_kv_tiles(key, part):
    span = 2 * REACH + 1
    offsets = jnp.arange(span) - REACH
    tiles = jnp.arange(NTILES)
    candidates = tiles[:, None] + offsets[None, :]
    usable = (candidates >= 0) & (candidates < NTILES) & (offsets[None, :] != 0)
    scores = jax.random.randint(jax.random.fold_in(key, 7), (NTILES, span), 0, 1 << 20)
    scores = scores * span + jnp.arange(span)[None, :]
    scores = jnp.where(usable, scores, -1 - jnp.arange(span)[None, :])
    picked = lax.top_k(scores, WIN - 1)[1]
    chosen = jnp.take_along_axis(candidates, picked, axis=1)
    return jnp.concatenate([tiles[:, None], chosen], axis=1).astype(jnp.int32)


def levels(key, shape, split, low, largest):
    factor_of = 1.0
    for axis_at, blocks in split:
        steps = jax.random.uniform(jax.random.fold_in(jax.random.fold_in(key, 6), axis_at), (blocks,), jnp.float32, low / len(split), largest / len(split))
        factor_of = factor_of * jnp.repeat(jnp.exp(steps), shape[axis_at] // blocks).reshape((-1,) + (1,) * (len(shape) - 1 - axis_at))
    return factor_of


def length_profile(amount, total, bound, skew):
    portions = [(1 << 20) // math.isqrt(rank ** skew) + 1 for rank in range(2, amount + 1)]
    surplus, holding = total - bound - (amount - 1), [1] * (amount - 1)
    while surplus > 0:
        movable = [i for i in range(amount - 1) if holding[i] < bound]
        whole, left = sum([portions[i] for i in movable]), surplus
        for i in movable:
            extra = min(bound - holding[i], max(1, left * portions[i] // whole), surplus)
            holding[i] = holding[i] + extra
            surplus = surplus - extra
    return np.array([bound] + holding)


def ragged(rng, count, total, bound, slope):
    if count == 2:
        one = jax.random.randint(rng, (), max(1, total - bound), min(bound, total - 1) + 1)
        return jnp.stack([one, total - one])
    sizes = jnp.asarray(length_profile(count, total, bound, slope), jnp.int32)
    twos = (count - 1) // 2
    donor, sink = sizes[1:1 + 2 * twos:2], sizes[2:2 + 2 * twos:2]
    slack = jnp.minimum(donor - 1, bound - sink)
    moved = jax.random.randint(jax.random.fold_in(rng, 1), (twos,), 0, 1 << 20) % (slack + 1)
    sizes = sizes.at[1:1 + 2 * twos:2].set(donor - moved).at[2:2 + 2 * twos:2].set(sink + moved)
    return sizes[jax.random.permutation(jax.random.fold_in(rng, 2), count)]


def scatter_about(key, dims, deviation, bound, cuts=(), dtype=jnp.bfloat16):
    values = jax.random.normal(key, dims, jnp.float32) * deviation
    if len(cuts) > 0:
        values = levels(key, dims, cuts, -0.22, 0.18) * values
    return jnp.clip(values, min=-bound, max=bound).astype(dtype)


def setup_inputs(seed: int = 0) -> dict:
    arg_keys = jax.random.split(jax.random.key(seed), 10)
    queries = draw_queries(jax.random.fold_in(arg_keys[9], 71), 0)
    keys = draw_keys(jax.random.fold_in(arg_keys[9], 71), 0)
    values = scatter_about(arg_keys[2], (GROUPS, N_BLK * T_DEV, HD), 1.0, 6.0, ((0, 2), (1, 16)))
    q_gain = jnp.clip(1.0 + 0.18 * jax.random.normal(arg_keys[3], (HD,), jnp.float32), 0.1, 1.9)
    k_gain = jnp.clip(1.0 + 0.18 * jax.random.normal(arg_keys[4], (HD,), jnp.float32), 0.1, 1.9)
    slopes = jnp.clip(jnp.exp(math.log(4.0) - 2.7725887 * jax.random.uniform(arg_keys[5], (HEADS,), jnp.float32) ** levels(arg_keys[5], (HEADS,), ((0, 2),), -0.2, 0.2)), 0.25, 4.0)
    out_weight = scatter_about(arg_keys[6], (HD, D), (HDIM // 4) ** -0.5, 1.0, ((0, 2), (1, 16)))
    kv_tiles = draw_kv_tiles(jax.random.fold_in(arg_keys[9], 71), 0)
    tile_frame = jnp.searchsorted(jnp.cumsum(ragged(arg_keys[8], FRAMES, NTILES, 16, 2)), jnp.arange(NTILES), side="right").astype(jnp.int32)
    return {"queries": queries, "keys": keys, "values": values, "q_gain": q_gain, "k_gain": k_gain, "slopes": slopes, "out_weight": out_weight, "kv_tiles": kv_tiles, "tile_frame": tile_frame}


def rms_norm(rows, gain):
    floats = rows.astype(jnp.float32)
    factor = lax.rsqrt(lax.optimization_barrier(jnp.mean(floats * floats, axis=-1, keepdims=True)) + 1e-06)
    return (floats * factor * gain).astype(jnp.bfloat16)

def to_sequence(array):
    groups, rows, width = array.shape
    return array.reshape(groups, N_BLK, rows // N_BLK, width).transpose(1, 0, 2, 3).reshape(groups * rows, width)

def reference(queries, keys, values, q_gain, k_gain, slopes, out_weight, kv_tiles, tile_frame):
    query_tiles = to_sequence(rms_norm(queries, q_gain)).reshape(NTILES, TILE, HEADS, HDIM)
    key_tiles = to_sequence(rms_norm(keys, k_gain)).reshape(NTILES, TILE, HEADS, HDIM)
    value_tiles = to_sequence(values).reshape(NTILES, TILE, HEADS, HDIM)

    def one_tile(tile):
        listed = kv_tiles[tile]
        near_keys = key_tiles[listed].reshape(WIN * TILE, HEADS, HDIM).astype(jnp.float32)
        near_values = value_tiles[listed].reshape(WIN * TILE, HEADS, HDIM).astype(jnp.float32)
        score = jnp.einsum('qhd,khd->hqk', query_tiles[tile].astype(jnp.float32), near_keys) * HDIM ** (-0.5)
        frame_gap = jnp.abs(tile_frame[tile] - tile_frame[listed]).astype(jnp.float32)
        penalty = slopes[:, None] * frame_gap[None, :]
        score = (score.reshape(HEADS, TILE, WIN, TILE) - penalty[:, None, :, None]).reshape(HEADS, TILE, WIN * TILE)
        weight = jnp.exp(score - lax.optimization_barrier(jnp.max(score, axis=-1, keepdims=True)))
        total = lax.optimization_barrier(jnp.sum(weight, axis=-1))
        rounded = weight.astype(jnp.bfloat16).astype(jnp.float32)
        summed = jnp.einsum('hqk,khd->qhd', rounded, near_values)
        return (summed / jnp.transpose(total)[:, :, None]).astype(jnp.bfloat16)
    attended = lax.map(one_tile, jnp.arange(NTILES)).reshape(TOKENS, HD)
    group_width = HD // N_HEAD
    mixed = jnp.zeros((TOKENS, D), jnp.float32)
    for group in range(N_HEAD):
        columns = attended[:, group * group_width:(group + 1) * group_width]
        weight_rows = out_weight[group * group_width:(group + 1) * group_width]
        partial_value = jnp.dot(columns, weight_rows, preferred_element_type=jnp.float32).astype(jnp.bfloat16)
        partial_value = lax.optimization_barrier(partial_value)
        mixed = mixed + partial_value.astype(jnp.float32)
    mixed = mixed.astype(jnp.bfloat16)
    return mixed.reshape(N_BLK, GROUPS, T_DEV, D).transpose(1, 0, 2, 3).reshape(GROUPS, N_BLK * T_DEV, D)
```

```python
import math

import jax
import jax.numpy as jnp
from jax import lax
from jax.experimental import pallas as pl
from jax.experimental.pallas import tpu as pltpu
from jax.sharding import PartitionSpec as P

HDIM = 128
TILE = 384
REACH = 3
LOG2E = math.log2(math.e)
CHUNKS = 4
TEAM = 8
STEP = 2
LINE = 4
PIECES = 5
NORM_ROWS = 64
NORM_GROUP = 16
MESH = pl.DeviceIdType.MESH
FLIPS = ((1, 0, 0), (0, 1, 0), (1, 0, 1), (0, 1, 1), (1, 1, 0), (1, 1, 1), (0, 0, 1))
VMEM_LIMIT = 60 * 1024 * 1024


def fused_kernel(sizes, index_ref, penalty_ref, q_gain_ref, k_gain_ref, q_ref, k_ref, v_ref, w_ref, out_ref, *scratch):
    planes, hpd, length, pair = sizes
    wins = REACH + 1
    slabs = TEAM * hpd
    per_tile = pair // HDIM
    frame = w_ref.shape[1]
    base = frame - HDIM
    inner = w_ref.shape[0]
    key_wins, value_wins = scratch[:hpd], scratch[hpd : 2 * hpd]
    (queries, keys_n, queries_n, gathered, weight, arrived, raw) = scratch[2 * hpd : 2 * hpd + 7]
    (
        raw_sem,
        qkv_send,
        qkv_recv,
        qkv_local,
        halo_send,
        halo_recv,
        w_send,
        w_recv,
        w_local,
        att_send,
        att_recv,
        att_local,
        x_send,
        x_recv,
        y_send,
        y_recv,
        out_local,
    ) = scratch[2 * hpd + 7 :]

    x, b = lax.axis_index("head"), lax.axis_index("blk")
    z, m = b // LINE, b % LINE
    y, c = m // 2, m % 2
    me = m * 2 + x

    def device(xx, zz, mm):
        return (xx, zz * LINE + mm)

    def remote(src, dst, send, recv, target):
        copy = pltpu.make_async_remote_copy(
            src_ref=src, dst_ref=dst, send_sem=send, recv_sem=recv, device_id=target, device_id_type=MESH
        )
        copy.start()

    def local(src, dst, sem):
        pltpu.make_async_copy(src, dst, sem).start()

    def wait(like, sem):
        pltpu.make_async_copy(like, like, sem).wait()

    def lanes(at):
        return pl.ds(pl.multiple_of(at * HDIM, HDIM), HDIM)

    mates = []
    for dx, dy, dc in FLIPS:
        mates.append(((x + dx) % 2, ((y + dy) % 2) * 2 + (c + dc) % 2))
    planes_off = [(z + k) % planes for k in range(1, planes)]

    barrier = pltpu.get_barrier_semaphore()
    for xx, mm in mates:
        pl.semaphore_signal(barrier, inc=1, device_id=device(xx, z, mm), device_id_type=MESH)
    for zz in planes_off:
        pl.semaphore_signal(barrier, inc=1, device_id=device(x, zz, m), device_id_type=MESH)
    pl.semaphore_wait(barrier, len(mates) + len(planes_off))

    rail = pl.ds(pl.multiple_of(c * frame, HDIM), frame)
    sibling = device(x, z, y * 2 + 1 - c)

    def weight_piece(piece):
        rows = pl.ds(piece * (inner // PIECES), inner // PIECES)
        for k, zz in enumerate(planes_off):
            remote(w_ref.at[rows], weight.at[z, rows, rail], w_send.at[k], w_recv.at[z * 2 + c], device(x, zz, m))

    def weight_forward(zz):
        wait(weight.at[zz, :, rail], w_recv.at[zz * 2 + c])
        remote(weight.at[zz, :, rail], weight.at[zz, :, rail], w_send.at[planes], w_recv.at[zz * 2 + c], sibling)

    local(w_ref, weight.at[z, :, rail], w_local)
    remote(w_ref, weight.at[z, :, rail], w_send.at[planes - 1], w_recv.at[z * 2 + c], sibling)

    def scatter(kind, h, source, window, at):
        for xx, mm in mates:
            head = (xx * LINE + mm) * hpd + h
            remote(source(head), window.at[at], qkv_send.at[kind], qkv_recv.at[kind, h], device(xx, z, mm))
        local(source((x * LINE + m) * hpd + h), window.at[at], qkv_local.at[kind, h])

    for h in range(hpd):
        scatter(0, h, lambda head: v_ref.at[0, :, lanes(head)], value_wins[h], REACH + me)

    def normed(source, gain_ref, target):
        steps = length // NORM_ROWS

        def chunk(step, slot):
            return pltpu.make_async_copy(
                source.at[0, pl.ds(step * NORM_ROWS, NORM_ROWS)], raw.at[slot], raw_sem.at[slot]
            )

        chunk(0, 0).start()

        @pl.loop(0, steps)
        def _(step):
            slot = step % 2

            @pl.when(step + 1 < steps)
            def _():
                chunk(step + 1, 1 - slot).start()

            chunk(step, slot).wait()

            @pl.loop(0, NORM_ROWS // NORM_GROUP)
            def _(group):
                floats = raw[slot, pl.ds(group * NORM_GROUP, NORM_GROUP), :].astype(jnp.float32)
                factor = lax.rsqrt(jnp.mean(floats * floats, axis=-1, keepdims=True) + 1e-06)
                rows = (floats * factor * gain_ref[...]).astype(jnp.bfloat16)
                at = pl.ds(step * NORM_ROWS + group * NORM_GROUP, NORM_GROUP)
                for slab in range(slabs):
                    target[slab, at, :] = rows[:, slab * HDIM : (slab + 1) * HDIM]

    normed(k_ref, k_gain_ref, keys_n)
    normed(q_ref, q_gain_ref, queries_n)
    for h in range(hpd):
        scatter(1, h, lambda head: keys_n.at[head], key_wins[h], REACH + me)
        scatter(2, h, lambda head: queries_n.at[head], queries.at[h], me)
    weight_piece(0)

    def landed(kind, h, window, first):
        own = window.at[pl.ds(first, TEAM - 1)]
        wait(own, qkv_recv.at[kind, h])
        wait(window.at[first], qkv_local.at[kind, h])

    top = REACH + TEAM

    def spread(kind, h, window):
        landed(kind, h, window, REACH)

        @pl.when(z < planes - 1)
        def _():
            remote(
                window.at[pl.ds(TEAM, REACH)],
                window.at[pl.ds(0, REACH)],
                halo_send.at[kind, 0, h],
                halo_recv.at[kind, 0, h],
                device(x, z + 1, m),
            )

        @pl.when(z > 0)
        def _():
            remote(
                window.at[pl.ds(REACH, REACH)],
                window.at[pl.ds(top, REACH)],
                halo_send.at[kind, 1, h],
                halo_recv.at[kind, 1, h],
                device(x, z - 1, m),
            )

    def halo_landed(h):
        for kind, window in ((0, value_wins[h]), (1, key_wins[h])):

            @pl.when(z > 0)
            def _():
                wait(window.at[pl.ds(0, REACH)], halo_recv.at[kind, 0, h])

            @pl.when(z < planes - 1)
            def _():
                wait(window.at[pl.ds(top, REACH)], halo_recv.at[kind, 1, h])

    def attend(h):
        halo_landed(h)

        @pl.loop(0, TEAM)
        def _(i):
            part, mm = i // LINE, i % LINE
            tile = mm * 2 + (x + 1 - part) % 2
            query = queries[h, tile]
            scores = []
            largest = None
            for win in range(wins):
                near = key_wins[h][index_ref[tile * wins + win]]
                score = lax.dot_general(
                    query, near, (((1,), (1,)), ((), ())), preferred_element_type=jnp.float32
                )
                penalty = penalty_ref[(h * TEAM + tile) * wins + win]
                most = jnp.max(score, axis=-1, keepdims=True) - penalty
                largest = most if largest is None else jnp.maximum(largest, most)
                scores.append((score, penalty))
            total = jnp.zeros((length, 1), jnp.float32)
            summed = jnp.zeros((length, HDIM), jnp.float32)
            for win, (score, penalty) in enumerate(scores):
                share = jnp.exp2(score - (largest + penalty))
                total += jnp.sum(share, axis=-1, keepdims=True)
                summed += jnp.dot(
                    share.astype(jnp.bfloat16),
                    value_wins[h][index_ref[tile * wins + win]],
                    preferred_element_type=jnp.float32,
                )
            queries[h, tile] = (summed / total).astype(jnp.bfloat16)
            there = gathered.at[part * 2 + mm // 2, :, lanes(m * hpd + h)]
            core = mm % 2
            remote(
                queries.at[h, tile], there, att_send.at[0], att_recv.at[part], device(x, z, (1 - y) * 2 + core)
            )

            @pl.when(core == c)
            def _():
                local(queries.at[h, tile], there, att_local.at[part])

            @pl.when(core != c)
            def _():
                remote(queries.at[h, tile], there, att_send.at[1], att_recv.at[part], sibling)

    for h in range(hpd):
        spread(0, h, value_wins[h])
    for piece in range(1, 3):
        weight_piece(piece)
    for h in range(hpd):
        spread(1, h, key_wins[h])
        landed(2, h, queries.at[h], 0)
        if h == 1:
            weight_piece(3)
        if h == 2:
            weight_piece(4)
        if h > 0:
            attend(h - 1)
    attend(hpd - 1)

    wait(keys_n.at[pl.ds(0, (TEAM - 1) * hpd)], qkv_send.at[1])
    wait(queries_n.at[pl.ds(0, (TEAM - 1) * hpd)], qkv_send.at[2])

    def near_plane(k):
        if k == 0:
            return z
        if planes == 4:
            low, high = z % 2, z // 2
            return (high + k // 2) % 2 * 2 + (low + k % 2) % 2
        return (z + k) % planes

    def project(part, row, zz):
        own = gathered[part * 2 + row]
        for start, width in ((0, base), (base, 2 * HDIM), (base + 2 * HDIM, base)):
            product = jnp.dot(own, weight[zz, :, start : start + width], preferred_element_type=jnp.float32)
            if start == base:
                yield base // HDIM, product[:, :HDIM] + product[:, HDIM:]
            else:
                first = start // HDIM if start < base else start // HDIM - 1
                for at in range(width // HDIM):
                    yield first + at, product[:, at * HDIM : (at + 1) * HDIM]

    def attended_landed(part):
        wait(keys_n.at[pl.ds(0, 2 * (LINE - 1) * hpd)], att_recv.at[part])
        wait(keys_n.at[pl.ds(0, 2 * hpd)], att_local.at[part])

    attended_landed(0)
    per_plane = 2 * per_tile
    for k in range(planes):
        zz = near_plane(k)
        if k == 0:
            wait(weight.at[zz, :, rail], w_local)
        else:
            weight_forward(zz)
        rest = pl.ds(pl.multiple_of((1 - c) * frame, HDIM), frame)
        wait(weight.at[zz, :, rest], w_recv.at[zz * 2 + 1 - c])

        @pl.loop(0, 2)
        def _(row):
            for slab, product in project(0, row, zz):
                keys_n[k * per_plane + row * per_tile + slab] = product.astype(jnp.bfloat16)

        remote(
            keys_n.at[pl.ds(k * per_plane, per_plane)],
            arrived.at[k],
            x_send.at[k],
            x_recv.at[k],
            device(1 - x, z, m),
        )

    attended_landed(1)
    for k in range(planes):
        zz = near_plane(k)
        wait(arrived.at[k], x_recv.at[k])

        @pl.loop(0, 2)
        def _(turn):
            row = (turn + 1 - y) % 2
            for slab, product in project(1, row, zz):
                floats = product + arrived[k, row * per_tile + slab].astype(jnp.float32)
                queries_n[k * per_plane + row * per_tile + slab] = floats.astype(jnp.bfloat16)
            for slab in range(per_tile):
                source = queries_n.at[k * per_plane + row * per_tile + slab]
                there = out_ref.at[0, :, lanes((zz * 2 + y) * per_tile + slab)]

                @pl.when(row == y)
                def _():
                    local(source, there, out_local)

                @pl.when(row != y)
                def _():
                    remote(source, there, y_send, y_recv, device(x, z, (1 - y) * 2 + c))

    half = planes * per_tile
    wait(queries_n.at[pl.ds(0, half)], y_recv)
    wait(queries_n.at[pl.ds(0, half)], out_local)
    wait(queries_n.at[pl.ds(0, half)], y_send)
    for k in range(planes):
        wait(arrived.at[k], x_send.at[k])
    wait(keys_n.at[pl.ds(0, (TEAM - 1) * hpd)], qkv_send.at[0])
    wait(keys_n, att_send.at[0])
    wait(keys_n.at[pl.ds(0, LINE * hpd)], att_send.at[1])
    for k in range(planes):
        wait(w_ref, w_send.at[k])
    wait(weight.at[pl.ds(0, planes - 1), :, rail], w_send.at[planes])
    for h in range(hpd):
        for kind, window in ((0, value_wins[h]), (1, key_wins[h])):

            @pl.when(z < planes - 1)
            def _():
                wait(window.at[pl.ds(0, REACH)], halo_send.at[kind, 0, h])

            @pl.when(z > 0)
            def _():
                wait(window.at[pl.ds(0, REACH)], halo_send.at[kind, 1, h])


def fused_shards(queries, keys, values, q_gain, k_gain, slopes, out_weight, kv_tiles, tile_frame):
    blocks = lax.axis_size("blk")
    position = lax.axis_index("blk")
    planes, member = blocks // LINE, lax.rem(position, LINE)
    length, features = values.shape[1:]
    hpd = features // (TEAM * HDIM)
    inner, narrow = out_weight.shape
    pair, frame = 2 * narrow, narrow + HDIM // 2

    start = position // LINE * TEAM
    listed = lax.dynamic_slice_in_dim(kv_tiles, start, TEAM, 0)
    own_frames = lax.dynamic_slice_in_dim(tile_frame, start, TEAM, 0)
    gap = jnp.abs(own_frames[:, None] - jnp.take(tile_frame, listed, axis=0)).astype(jnp.float32)
    own_slopes = lax.dynamic_slice_in_dim(slopes, member * hpd, hpd, 0)
    penalty = (own_slopes * LOG2E)[:, None] * gap.reshape(1, -1)
    index = (listed - (start - REACH)).reshape(-1)

    framed = jnp.where(
        position % 2 == 0,
        jnp.pad(out_weight, ((0, 0), (0, HDIM // 2))),
        jnp.pad(out_weight, ((0, 0), (HDIM // 2, 0))),
    )

    def body(*refs):
        fused_kernel((planes, hpd, length, pair), *refs)

    dma, half = pltpu.SemaphoreType.DMA, jnp.bfloat16
    slabs = TEAM * hpd
    anywhere = pl.BlockSpec(memory_space=pl.ANY)
    smem = pl.BlockSpec(memory_space=pltpu.SMEM)
    vmem = pl.BlockSpec(memory_space=pltpu.VMEM)
    window = pltpu.VMEM((TEAM + 2 * REACH, length, HDIM), half)
    rows = TEAM * length
    return pl.pallas_call(
        body,
        in_specs=[smem, smem, vmem, vmem, anywhere, anywhere, anywhere, anywhere],
        out_specs=anywhere,
        out_shape=jax.ShapeDtypeStruct((1, length, narrow * blocks), half),
        scratch_shapes=[window] * (2 * hpd)
        + [
            pltpu.VMEM((hpd, TEAM, length, HDIM), half),
            pltpu.VMEM((slabs, length, HDIM), half),
            pltpu.VMEM((slabs, length, HDIM), half),
            pltpu.VMEM((4, length, inner), half),
            pltpu.VMEM((planes, inner, 2 * frame), half),
            pltpu.VMEM((planes, 2 * pair // HDIM, length, HDIM), half),
            pltpu.VMEM((2, NORM_ROWS, features), half),
            dma((2,)),
            dma((3,)),
            dma((3, hpd)),
            dma((3, hpd)),
            dma((2, 2, hpd)),
            dma((2, 2, hpd)),
            dma((planes + 1,)),
            dma((2 * planes,)),
            dma,
            dma((2,)),
            dma((2,)),
            dma((2,)),
            dma((planes,)),
            dma((planes,)),
            dma,
            dma,
            dma,
        ],
        compiler_params=pltpu.CompilerParams(
            vmem_limit_bytes=VMEM_LIMIT, collective_id=0, has_side_effects=True
        ),
        cost_estimate=pl.CostEstimate(
            flops=4 * rows * (REACH + 1) * TILE * hpd * HDIM + 4 * length * inner * narrow * blocks,
            bytes_accessed=8 * length * features + 2 * inner * narrow,
            transcendentals=rows * (REACH + 1) * TILE * hpd,
        ),
    )(
        index,
        penalty.reshape(-1),
        (q_gain * (LOG2E * HDIM ** (-0.5)))[None],
        k_gain[None],
        queries,
        keys,
        values,
        framed,
    )


def shifted(value, axis, steps):
    count = lax.axis_size(axis)
    initial, last = (max(0, -steps), min(count, count - steps))
    return lax.ppermute(value, axis, [(source, source + steps) for source in range(initial, last)])


def rms_norm(rows, gain):
    floats = rows.astype(jnp.float32)
    factor = lax.rsqrt(jnp.mean(floats * floats, axis=-1, keepdims=True) + 1e-06)
    return (floats * factor * gain).astype(jnp.bfloat16)


def attend_kernel(tiles, wins, parts, index_ref, penalty_ref, *refs):
    q_ref = refs[0]
    key_refs = refs[1 : 1 + parts]
    value_refs = refs[1 + parts : 1 + 2 * parts]
    out_ref, key_window, value_window = refs[1 + 2 * parts :]
    head = pl.program_id(0)
    first = pl.program_id(1) * STEP

    @pl.when(first == 0)
    def _():
        for window, blocks in ((key_window, key_refs), (value_window, value_refs)):
            at = 0
            for block in blocks:
                for tile in range(block.shape[0] // TILE):
                    window[at] = block[tile * TILE : (tile + 1) * TILE, :]
                    at += 1

    for step in range(STEP):
        tile = first + step
        query = q_ref[step * TILE : (step + 1) * TILE, :]
        scores = []
        largest = None
        for win in range(wins):
            near = key_window[index_ref[tile * wins + win]]
            score = lax.dot_general(
                query, near, (((1,), (1,)), ((), ())), preferred_element_type=jnp.float32
            )
            penalty = penalty_ref[(head * tiles + tile) * wins + win]
            top = jnp.max(score, axis=-1, keepdims=True) - penalty
            largest = top if largest is None else jnp.maximum(largest, top)
            scores.append((score, penalty))
        total = jnp.zeros((TILE, 1), jnp.float32)
        summed = jnp.zeros((TILE, HDIM), jnp.float32)
        for win, (score, penalty) in enumerate(scores):
            weight = jnp.exp2(score - (largest + penalty))
            total += jnp.sum(weight, axis=-1, keepdims=True)
            summed += jnp.dot(
                weight.astype(jnp.bfloat16),
                value_window[index_ref[tile * wins + win]],
                preferred_element_type=jnp.float32,
            )
        out_ref[step * TILE : (step + 1) * TILE, :] = (summed / total).astype(out_ref.dtype)


def attend(query, key_parts, value_parts, index, penalty):
    rows, width = query.shape
    heads, tiles, wins = width // HDIM, rows // TILE, index.shape[0] * TILE // rows
    window = sum(part.shape[0] for part in key_parts) // TILE

    def column(array):
        return pl.BlockSpec((array.shape[0], HDIM), lambda h, t, *_: (0, h))

    stepped = pl.BlockSpec((STEP * TILE, HDIM), lambda h, t, *_: (t, h))

    def body(*refs):
        attend_kernel(tiles, wins, len(key_parts), *refs)

    operands = (query, *key_parts, *value_parts)
    return pl.pallas_call(
        body,
        grid_spec=pltpu.PrefetchScalarGridSpec(
            num_scalar_prefetch=2,
            grid=(heads, tiles // STEP),
            in_specs=[stepped, *(column(array) for array in operands[1:])],
            out_specs=stepped,
            scratch_shapes=[pltpu.VMEM((window, TILE, HDIM), jnp.bfloat16)] * 2,
        ),
        out_shape=jax.ShapeDtypeStruct(query.shape, jnp.bfloat16),
        compiler_params=pltpu.CompilerParams(vmem_limit_bytes=48 * 1024 * 1024),
        cost_estimate=pl.CostEstimate(
            flops=4 * rows * wins * TILE * width,
            bytes_accessed=2 * sum(array.size for array in operands) + 2 * query.size,
            transcendentals=rows * wins * TILE * heads,
        ),
    )(index, penalty, *operands)


def halo(own, hop):
    reach = REACH * TILE
    lower = shifted(own[own.shape[0] - reach :], "blk", hop)
    upper = shifted(own[:reach], "blk", -hop)
    return [lower, own, upper]


def general_shards(queries, keys, values, q_gain, k_gain, slopes, out_weight, kv_tiles, tile_frame):
    groups, blocks = lax.axis_size("head"), lax.axis_size("blk")
    position, group = lax.axis_index("blk"), lax.axis_index("head")
    hop = TEAM // groups
    member = lax.rem(position, hop)
    teams = [
        [head * blocks + first + inner for inner in range(hop) for head in range(groups)]
        for first in range(0, blocks, hop)
    ]
    lines = [list(range(first, first + hop)) for first in range(0, blocks, hop)]
    length, features = values.shape[1:]
    narrow = features // TEAM

    def to_heads(rows):
        parts = rows.reshape(length, groups, hop, narrow).transpose(2, 1, 0, 3)
        parts = lax.all_to_all(
            parts.reshape(TEAM, length, narrow),
            ("head", "blk"),
            split_axis=0,
            concat_axis=0,
            axis_index_groups=teams,
            tiled=True,
        )
        return parts.reshape(TEAM * length, narrow)

    full_columns = lax.all_gather(out_weight, "blk", axis=1, tiled=True)
    value_own = to_heads(values[0])
    key_own = to_heads(rms_norm(keys[0], k_gain))
    value_parts = halo(value_own, hop)
    query_normed = rms_norm(queries[0], q_gain * (LOG2E * HDIM ** (-0.5)))
    query_normed, value_parts[0], value_parts[2] = lax.optimization_barrier(
        (query_normed, value_parts[0], value_parts[2])
    )
    query_own = to_heads(query_normed)
    tiles = query_own.shape[0] // TILE
    key_parts = halo(key_own, hop)

    start = position // hop * tiles
    listed = lax.dynamic_slice_in_dim(kv_tiles, start, tiles, 0)
    own_frames = lax.dynamic_slice_in_dim(tile_frame, start, tiles, 0)
    gap = jnp.abs(own_frames[:, None] - jnp.take(tile_frame, listed, axis=0)).astype(jnp.float32)
    heads = narrow // HDIM
    own_slopes = lax.dynamic_slice_in_dim(slopes, member * heads, heads, 0)
    penalty = (own_slopes * LOG2E)[:, None] * gap.reshape(1, -1)
    index = (listed - (start - REACH)).reshape(-1)
    attended = attend(query_own, key_parts, value_parts, index, penalty.reshape(-1))
    attended = lax.all_to_all(
        attended.reshape(hop, groups * length, narrow),
        "blk",
        split_axis=0,
        concat_axis=0,
        axis_index_groups=lines,
        tiled=True,
    )
    attended = attended.transpose(1, 0, 2).reshape(groups * length, hop * narrow)

    rows = attended.shape[0] // groups
    width = full_columns.shape[1] // CHUNKS

    def partial(owner, chunk):
        return jnp.dot(
            lax.dynamic_slice_in_dim(attended, owner * rows, rows, 0),
            full_columns[:, chunk * width : (chunk + 1) * width],
            preferred_element_type=jnp.float32,
        ).astype(jnp.bfloat16)

    arrived = []
    for chunk in range(CHUNKS):
        arrived.append(
            [
                lax.ppermute(
                    partial(lax.rem(group + step, groups), chunk),
                    "head",
                    [(source, (source + step) % groups) for source in range(groups)],
                )
                for step in range(1, groups)
            ]
        )
    mixed = []
    for chunk in range(CHUNKS):
        floats = partial(group, chunk).astype(jnp.float32)
        for term in arrived[chunk]:
            floats = floats + term.astype(jnp.float32)
        mixed.append(floats.astype(jnp.bfloat16))
    return jnp.concatenate(mixed, axis=1)[None]


def shards(*arrays):
    queries, out_weight = arrays[0], arrays[6]
    rows = queries.shape[1]
    if lax.axis_size("head") == 2 and lax.axis_size("blk") % LINE == 0 and rows == TILE:
        if out_weight.shape[1] % HDIM == HDIM // 2:
            return fused_shards(*arrays)
    return general_shards(*arrays)


def solution(mesh):
    placed = (
        P("head", "blk", None),
        P("head", "blk", None),
        P("head", "blk", None),
        P(),
        P(),
        P("head"),
        P("head", "blk"),
        P(),
        P(),
    )
    return jax.shard_map(
        shards, mesh=mesh, in_specs=placed, out_specs=P("head", "blk", None), check_vma=False
    )
```

```python
import math

import jax
import jax.numpy as jnp
from jax import lax
from jax.experimental import pallas as pl
from jax.experimental.pallas import tpu as pltpu
from jax.sharding import PartitionSpec as P

HDIM = 128
TILE = 384
REACH = 3
LOG2E = math.log2(math.e)
CHUNKS = 4
TEAM = 8
STEP = 2
LINE = 4
NORM_ROWS = 64
NORM_GROUP = 16
MESH = pl.DeviceIdType.MESH
FLIPS = ((1, 0, 0), (0, 1, 0), (1, 0, 1), (0, 1, 1), (1, 1, 0), (1, 1, 1), (0, 0, 1))
VMEM_LIMIT = 60 * 1024 * 1024


def fused_kernel(sizes, near_ref, frame_ref, slope_ref, q_gain_ref, k_gain_ref, q_ref, k_ref, v_ref, w_ref, out_ref, *scratch):
    planes, hpd, length, pair = sizes
    wins = REACH + 1
    slabs = TEAM * hpd
    per_tile = pair // HDIM
    narrow, inner = w_ref.shape
    key_wins, value_wins = scratch[:hpd], scratch[hpd : 2 * hpd]
    (queries, keys_n, queries_n, gathered, weight, arrived, raw) = scratch[2 * hpd : 2 * hpd + 7]
    (
        raw_sem,
        qkv_send,
        qkv_recv,
        qkv_local,
        halo_send,
        halo_recv,
        w_send,
        w_recv,
        w_local,
        att_send,
        att_recv,
        att_local,
        x_send,
        x_recv,
        y_send,
        y_recv,
        out_local,
    ) = scratch[2 * hpd + 7 :]

    x, b = lax.axis_index("head"), lax.axis_index("blk")
    z, m = b // LINE, b % LINE
    y, c = m // 2, m % 2
    me = m * 2 + x

    def device(xx, zz, mm):
        return (xx, zz * LINE + mm)

    def remote(src, dst, send, recv, target):
        copy = pltpu.make_async_remote_copy(
            src_ref=src, dst_ref=dst, send_sem=send, recv_sem=recv, device_id=target, device_id_type=MESH
        )
        copy.start()

    def local(src, dst, sem):
        pltpu.make_async_copy(src, dst, sem).start()

    def wait(like, sem):
        pltpu.make_async_copy(like, like, sem).wait()

    def lanes(at):
        return pl.ds(pl.multiple_of(at * HDIM, HDIM), HDIM)

    mates = []
    for dx, dy, dc in FLIPS:
        mates.append(((x + dx) % 2, ((y + dy) % 2) * 2 + (c + dc) % 2))
    planes_off = [(z + k) % planes for k in range(1, planes)]

    barrier = pltpu.get_barrier_semaphore()
    for xx, mm in mates:
        pl.semaphore_signal(barrier, inc=1, device_id=device(xx, z, mm), device_id_type=MESH)
    for zz in planes_off:
        pl.semaphore_signal(barrier, inc=1, device_id=device(x, zz, m), device_id_type=MESH)
    pl.semaphore_wait(barrier, len(mates) + len(planes_off))

    rail = pl.ds(pl.multiple_of(c * narrow, HDIM // 2), narrow)
    rest = pl.ds(pl.multiple_of((1 - c) * narrow, HDIM // 2), narrow)
    sibling = device(x, z, y * 2 + 1 - c)

    def weight_send(block, source, step):
        there = weight.at[block, rail]
        arrival = w_recv.at[block * 2 + c]
        if step >= 0:

            @pl.when(z < planes - 1)
            def _():
                remote(source, there, w_send.at[step, 0], arrival, device(x, z + 1, m))

        if step <= 0:

            @pl.when(z > 0)
            def _():
                remote(source, there, w_send.at[-step, 1], arrival, device(x, z - 1, m))

        remote(source, there, w_send.at[abs(step), 2 + (step < 0)], arrival, sibling)

    def weight_forward(step):
        for sign in (1, -1):

            @pl.when(z >= step if sign > 0 else z < planes - step)
            def _():
                block = z - sign * step
                wait(weight.at[block, rail], w_recv.at[block * 2 + c])
                weight_send(block, weight.at[block, rail], sign * step)

    def weight_left():
        @pl.when(z < planes - 1)
        def _():
            wait(w_ref, w_send.at[0, 0])

        @pl.when(z > 0)
        def _():
            wait(w_ref, w_send.at[0, 1])

        wait(w_ref, w_send.at[0, 2])
        for step in range(1, planes):
            for way in range(2):
                here = z >= step if way == 0 else z < planes - step
                onward = z < planes - 1 if way == 0 else z > 0

                @pl.when(here)
                def _():
                    wait(w_ref, w_send.at[step, 2 + way])

                @pl.when(here & onward)
                def _():
                    wait(w_ref, w_send.at[step, way])

    local(w_ref, weight.at[z, rail], w_local)
    weight_send(z, w_ref, 0)

    def scatter(kind, h, source, window, at, side=None):
        for (xx, mm), (dx, _, _) in zip(mates, FLIPS):
            if side is None or side == dx:
                head = (xx * LINE + mm) * hpd + h
                slot = kind + 1 if side == 0 else kind
                remote(source(head), window.at[at], qkv_send.at[slot], qkv_recv.at[slot, h], device(xx, z, mm))
        if side != 1:
            local(source((x * LINE + m) * hpd + h), window.at[at], qkv_local.at[kind, h])

    for h in range(hpd):
        scatter(0, h, lambda head: v_ref.at[0, :, lanes(head)], value_wins[h], REACH + me)

    def normed(source, gain_ref, scale, target):
        steps = length // NORM_ROWS

        def chunk(step, slot):
            return pltpu.make_async_copy(
                source.at[0, pl.ds(step * NORM_ROWS, NORM_ROWS)], raw.at[slot], raw_sem.at[slot]
            )

        chunk(0, 0).start()

        @pl.loop(0, steps)
        def _(step):
            slot = step % 2

            @pl.when(step + 1 < steps)
            def _():
                chunk(step + 1, 1 - slot).start()

            chunk(step, slot).wait()

            @pl.loop(0, NORM_ROWS // NORM_GROUP)
            def _(group):
                floats = raw[slot, pl.ds(group * NORM_GROUP, NORM_GROUP), :].astype(jnp.float32)
                factor = lax.rsqrt(jnp.mean(floats * floats, axis=-1, keepdims=True) + 1e-06)
                rows = (floats * (factor * scale) * gain_ref[...]).astype(jnp.bfloat16)
                at = pl.ds(step * NORM_ROWS + group * NORM_GROUP, NORM_GROUP)
                for slab in range(slabs):
                    target[slab, at, :] = rows[:, slab * HDIM : (slab + 1) * HDIM]

    normed(k_ref, k_gain_ref, 1.0, keys_n)
    normed(q_ref, q_gain_ref, LOG2E * HDIM ** (-0.5), queries_n)
    for h in range(hpd):
        scatter(1, h, lambda head: keys_n.at[head], key_wins[h], REACH + me)
        scatter(2, h, lambda head: queries_n.at[head], queries.at[h], me, 1)

    def landed(kind, h, window, first):
        wait(window.at[pl.ds(first, TEAM - 1)], qkv_recv.at[kind, h])
        wait(window.at[first], qkv_local.at[kind, h])

    top = REACH + TEAM

    def spread(kind, h, window):
        landed(kind, h, window, REACH)

        @pl.when(z < planes - 1)
        def _():
            remote(
                window.at[pl.ds(TEAM, REACH)],
                window.at[pl.ds(0, REACH)],
                halo_send.at[kind, 0, h],
                halo_recv.at[kind, 0, h],
                device(x, z + 1, m),
            )

        @pl.when(z > 0)
        def _():
            remote(
                window.at[pl.ds(REACH, REACH)],
                window.at[pl.ds(top, REACH)],
                halo_send.at[kind, 1, h],
                halo_recv.at[kind, 1, h],
                device(x, z - 1, m),
            )

    def halo_landed(h):
        for kind, window in ((0, value_wins[h]), (1, key_wins[h])):

            @pl.when(z > 0)
            def _():
                wait(window.at[pl.ds(0, REACH)], halo_recv.at[kind, 0, h])

            @pl.when(z < planes - 1)
            def _():
                wait(window.at[pl.ds(top, REACH)], halo_recv.at[kind, 1, h])

    def penalty(h, tile, near):
        gap = jnp.abs(frame_ref[tile] - frame_ref[near]).astype(jnp.float32)
        return slope_ref[m * hpd + h] * LOG2E * gap

    def attend(part, h):
        @pl.loop(0, LINE)
        def _(mm):
            tile = mm * 2 + (x + 1 - part) % 2
            at = z * TEAM + tile
            nears = [near_ref[at * wins + win] for win in range(wins)]
            slots = [jnp.clip(near - (z * TEAM - REACH), 0, TEAM + 2 * REACH - 1) for near in nears]
            query = queries[h, tile]
            scores = []
            largest = None
            for win in range(wins):
                near = key_wins[h][slots[win]]
                score = lax.dot_general(
                    query, near, (((1,), (1,)), ((), ())), preferred_element_type=jnp.float32
                )
                less = penalty(h, at, nears[win])
                most = jnp.max(score, axis=-1, keepdims=True) - less
                largest = most if largest is None else jnp.maximum(largest, most)
                scores.append((score, less))
            total = jnp.zeros((length, 1), jnp.float32)
            summed = jnp.zeros((length, HDIM), jnp.float32)
            for win, (score, less) in enumerate(scores):
                share = jnp.exp2(score - (largest + less))
                total += jnp.sum(share, axis=-1, keepdims=True)
                summed += jnp.dot(
                    share.astype(jnp.bfloat16),
                    value_wins[h][slots[win]],
                    preferred_element_type=jnp.float32,
                )
            queries[h, tile] = (summed / total).astype(jnp.bfloat16)
            there = gathered.at[part * 2 + mm // 2, :, lanes(m * hpd + h)]
            core = mm % 2
            remote(
                queries.at[h, tile], there, att_send.at[0], att_recv.at[part], device(x, z, (1 - y) * 2 + core)
            )

            @pl.when(core == c)
            def _():
                local(queries.at[h, tile], there, att_local.at[part])

            @pl.when(core != c)
            def _():
                remote(queries.at[h, tile], there, att_send.at[1], att_recv.at[part], sibling)

    for h in range(hpd):
        spread(0, h, value_wins[h])
    for h in range(hpd):
        spread(1, h, key_wins[h])
        wait(queries.at[h, pl.ds(0, LINE)], qkv_recv.at[2, h])
        if h == 2:
            weight_forward(1)
        if h > 0:
            halo_landed(h - 1)
            attend(0, h - 1)
    halo_landed(hpd - 1)
    attend(0, hpd - 1)
    for h in range(hpd):
        scatter(2, h, lambda head: queries_n.at[head], queries.at[h], me, 0)
    weight_forward(2)

    def attend_own(h):
        wait(queries.at[h, pl.ds(0, LINE - 1)], qkv_recv.at[3, h])
        wait(queries.at[h, 0], qkv_local.at[2, h])
        attend(1, h)

    wait(keys_n.at[pl.ds(0, (TEAM - 1) * hpd)], qkv_send.at[1])

    def near_plane(k):
        if k == 0:
            return z
        if planes == 4:
            low, high = z % 2, z // 2
            return (high + k // 2) % 2 * 2 + (low + k % 2) % 2
        return (z + k) % planes

    def project(part, zz, first, width):
        return lax.dot_general(
            gathered[part * 2 : part * 2 + 2].reshape(2 * length, inner),
            weight[zz, first : first + width, :],
            (((1,), (1,)), ((), ())),
            preferred_element_type=jnp.float32,
        )

    spans = [(first, min(2 * HDIM, pair - first)) for first in range(0, pair, 2 * HDIM)]

    def attended_landed(part):
        wait(keys_n.at[pl.ds(0, 2 * (LINE - 1) * hpd)], att_recv.at[part])
        wait(keys_n.at[pl.ds(0, 2 * hpd)], att_local.at[part])

    attended_landed(0)
    per_plane = 2 * per_tile
    turns = [k * hpd // planes for k in range(planes + 1)]
    for k in range(planes):
        zz = near_plane(k)
        if k == 0:
            wait(weight.at[zz, rail], w_local)
        if k == planes - 1:
            for step in range(3, planes):
                weight_forward(step)
        wait(weight.at[zz, rest], w_recv.at[zz * 2 + 1 - c])
        for first, width in spans:
            product = project(0, zz, first, width).astype(jnp.bfloat16)
            for row in range(2):
                for at in range(width // HDIM):
                    slab = k * per_plane + row * per_tile + first // HDIM + at
                    keys_n[slab] = product[row * length : (row + 1) * length, at * HDIM : (at + 1) * HDIM]
        remote(
            keys_n.at[pl.ds(k * per_plane, per_plane)],
            arrived.at[k],
            x_send.at[k],
            x_recv.at[k],
            device(1 - x, z, m),
        )
        for h in range(turns[k], turns[k + 1]):
            attend_own(h)

    wait(queries_n.at[pl.ds(0, LINE * hpd)], qkv_send.at[2])
    wait(queries_n.at[pl.ds(0, (LINE - 1) * hpd)], qkv_send.at[3])
    attended_landed(1)
    for k in range(planes):
        zz = near_plane(k)
        wait(arrived.at[k], x_recv.at[k])
        for first, width in spans:
            product = project(1, zz, first, width)
            for row in range(2):
                for at in range(width // HDIM):
                    lane = first // HDIM + at
                    slab = k * per_plane + row * per_tile + lane
                    floats = product[row * length : (row + 1) * length, at * HDIM : (at + 1) * HDIM]
                    floats = floats + arrived[k, row * per_tile + lane].astype(jnp.float32)
                    queries_n[slab] = floats.astype(jnp.bfloat16)

            @pl.loop(0, 2)
            def _(row):
                for at in range(width // HDIM):
                    lane = first // HDIM + at
                    source = queries_n.at[k * per_plane + row * per_tile + lane]
                    there = out_ref.at[0, :, lanes((zz * 2 + y) * per_tile + lane)]

                    @pl.when(row == y)
                    def _():
                        local(source, there, out_local)

                    @pl.when(row != y)
                    def _():
                        remote(source, there, y_send, y_recv, device(x, z, (1 - y) * 2 + c))

    half = planes * per_tile
    wait(queries_n.at[pl.ds(0, half)], y_recv)
    wait(queries_n.at[pl.ds(0, half)], out_local)
    wait(queries_n.at[pl.ds(0, half)], y_send)
    for k in range(planes):
        wait(arrived.at[k], x_send.at[k])
    wait(keys_n.at[pl.ds(0, (TEAM - 1) * hpd)], qkv_send.at[0])
    wait(keys_n, att_send.at[0])
    wait(keys_n.at[pl.ds(0, LINE * hpd)], att_send.at[1])
    weight_left()
    for h in range(hpd):
        for kind, window in ((0, value_wins[h]), (1, key_wins[h])):

            @pl.when(z < planes - 1)
            def _():
                wait(window.at[pl.ds(0, REACH)], halo_send.at[kind, 0, h])

            @pl.when(z > 0)
            def _():
                wait(window.at[pl.ds(0, REACH)], halo_send.at[kind, 1, h])


def fused_shards(queries, keys, values, q_gain, k_gain, slopes, out_weight, kv_tiles, tile_frame):
    blocks = lax.axis_size("blk")
    planes = blocks // LINE
    length, features = values.shape[1:]
    hpd = features // (TEAM * HDIM)
    inner, narrow = out_weight.shape
    pair = 2 * narrow

    def body(*refs):
        fused_kernel((planes, hpd, length, pair), *refs)

    dma, half = pltpu.SemaphoreType.DMA, jnp.bfloat16
    slabs = TEAM * hpd
    anywhere = pl.BlockSpec(memory_space=pl.ANY)
    smem = pl.BlockSpec(memory_space=pltpu.SMEM)
    vmem = pl.BlockSpec(memory_space=pltpu.VMEM)
    window = pltpu.VMEM((TEAM + 2 * REACH, length, HDIM), half)
    rows = TEAM * length
    return pl.pallas_call(
        body,
        in_specs=[smem, smem, smem, vmem, vmem, anywhere, anywhere, anywhere, anywhere],
        out_specs=anywhere,
        out_shape=jax.ShapeDtypeStruct((1, length, narrow * blocks), half),
        scratch_shapes=[window] * (2 * hpd)
        + [
            pltpu.VMEM((hpd, TEAM, length, HDIM), half),
            pltpu.VMEM((slabs, length, HDIM), half),
            pltpu.VMEM((slabs, length, HDIM), half),
            pltpu.VMEM((4, length, inner), half),
            pltpu.VMEM((planes, pair, inner), half),
            pltpu.VMEM((planes, 2 * pair // HDIM, length, HDIM), half),
            pltpu.VMEM((2, NORM_ROWS, features), half),
            dma((2,)),
            dma((4,)),
            dma((4, hpd)),
            dma((3, hpd)),
            dma((2, 2, hpd)),
            dma((2, 2, hpd)),
            dma((planes, 4)),
            dma((2 * planes,)),
            dma,
            dma((2,)),
            dma((2,)),
            dma((2,)),
            dma((planes,)),
            dma((planes,)),
            dma,
            dma,
            dma,
        ],
        compiler_params=pltpu.CompilerParams(
            vmem_limit_bytes=VMEM_LIMIT, collective_id=0, has_side_effects=True
        ),
        cost_estimate=pl.CostEstimate(
            flops=4 * rows * (REACH + 1) * TILE * hpd * HDIM + 4 * length * inner * narrow * blocks,
            bytes_accessed=8 * length * features + 2 * inner * narrow,
            transcendentals=rows * (REACH + 1) * TILE * hpd,
        ),
    )(
        kv_tiles.reshape(-1),
        tile_frame,
        slopes,
        q_gain[None],
        k_gain[None],
        queries,
        keys,
        values,
        out_weight.T,
    )


def shifted(value, axis, steps):
    count = lax.axis_size(axis)
    initial, last = (max(0, -steps), min(count, count - steps))
    return lax.ppermute(value, axis, [(source, source + steps) for source in range(initial, last)])


def rms_norm(rows, gain):
    floats = rows.astype(jnp.float32)
    factor = lax.rsqrt(jnp.mean(floats * floats, axis=-1, keepdims=True) + 1e-06)
    return (floats * factor * gain).astype(jnp.bfloat16)


def attend_kernel(tiles, wins, parts, index_ref, penalty_ref, *refs):
    q_ref = refs[0]
    key_refs = refs[1 : 1 + parts]
    value_refs = refs[1 + parts : 1 + 2 * parts]
    out_ref, key_window, value_window = refs[1 + 2 * parts :]
    head = pl.program_id(0)
    first = pl.program_id(1) * STEP

    @pl.when(first == 0)
    def _():
        for window, blocks in ((key_window, key_refs), (value_window, value_refs)):
            at = 0
            for block in blocks:
                for tile in range(block.shape[0] // TILE):
                    window[at] = block[tile * TILE : (tile + 1) * TILE, :]
                    at += 1

    for step in range(STEP):
        tile = first + step
        query = q_ref[step * TILE : (step + 1) * TILE, :]
        scores = []
        largest = None
        for win in range(wins):
            near = key_window[index_ref[tile * wins + win]]
            score = lax.dot_general(
                query, near, (((1,), (1,)), ((), ())), preferred_element_type=jnp.float32
            )
            penalty = penalty_ref[(head * tiles + tile) * wins + win]
            top = jnp.max(score, axis=-1, keepdims=True) - penalty
            largest = top if largest is None else jnp.maximum(largest, top)
            scores.append((score, penalty))
        total = jnp.zeros((TILE, 1), jnp.float32)
        summed = jnp.zeros((TILE, HDIM), jnp.float32)
        for win, (score, penalty) in enumerate(scores):
            weight = jnp.exp2(score - (largest + penalty))
            total += jnp.sum(weight, axis=-1, keepdims=True)
            summed += jnp.dot(
                weight.astype(jnp.bfloat16),
                value_window[index_ref[tile * wins + win]],
                preferred_element_type=jnp.float32,
            )
        out_ref[step * TILE : (step + 1) * TILE, :] = (summed / total).astype(out_ref.dtype)


def attend(query, key_parts, value_parts, index, penalty):
    rows, width = query.shape
    heads, tiles, wins = width // HDIM, rows // TILE, index.shape[0] * TILE // rows
    window = sum(part.shape[0] for part in key_parts) // TILE

    def column(array):
        return pl.BlockSpec((array.shape[0], HDIM), lambda h, t, *_: (0, h))

    stepped = pl.BlockSpec((STEP * TILE, HDIM), lambda h, t, *_: (t, h))

    def body(*refs):
        attend_kernel(tiles, wins, len(key_parts), *refs)

    operands = (query, *key_parts, *value_parts)
    return pl.pallas_call(
        body,
        grid_spec=pltpu.PrefetchScalarGridSpec(
            num_scalar_prefetch=2,
            grid=(heads, tiles // STEP),
            in_specs=[stepped, *(column(array) for array in operands[1:])],
            out_specs=stepped,
            scratch_shapes=[pltpu.VMEM((window, TILE, HDIM), jnp.bfloat16)] * 2,
        ),
        out_shape=jax.ShapeDtypeStruct(query.shape, jnp.bfloat16),
        compiler_params=pltpu.CompilerParams(vmem_limit_bytes=48 * 1024 * 1024),
        cost_estimate=pl.CostEstimate(
            flops=4 * rows * wins * TILE * width,
            bytes_accessed=2 * sum(array.size for array in operands) + 2 * query.size,
            transcendentals=rows * wins * TILE * heads,
        ),
    )(index, penalty, *operands)


def halo(own, hop):
    reach = REACH * TILE
    lower = shifted(own[own.shape[0] - reach :], "blk", hop)
    upper = shifted(own[:reach], "blk", -hop)
    return [lower, own, upper]


def general_shards(queries, keys, values, q_gain, k_gain, slopes, out_weight, kv_tiles, tile_frame):
    groups, blocks = lax.axis_size("head"), lax.axis_size("blk")
    position, group = lax.axis_index("blk"), lax.axis_index("head")
    hop = TEAM // groups
    member = lax.rem(position, hop)
    teams = [
        [head * blocks + first + inner for inner in range(hop) for head in range(groups)]
        for first in range(0, blocks, hop)
    ]
    lines = [list(range(first, first + hop)) for first in range(0, blocks, hop)]
    length, features = values.shape[1:]
    narrow = features // TEAM

    def to_heads(rows):
        parts = rows.reshape(length, groups, hop, narrow).transpose(2, 1, 0, 3)
        parts = lax.all_to_all(
            parts.reshape(TEAM, length, narrow),
            ("head", "blk"),
            split_axis=0,
            concat_axis=0,
            axis_index_groups=teams,
            tiled=True,
        )
        return parts.reshape(TEAM * length, narrow)

    full_columns = lax.all_gather(out_weight, "blk", axis=1, tiled=True)
    value_own = to_heads(values[0])
    key_own = to_heads(rms_norm(keys[0], k_gain))
    value_parts = halo(value_own, hop)
    query_normed = rms_norm(queries[0], q_gain * (LOG2E * HDIM ** (-0.5)))
    query_normed, value_parts[0], value_parts[2] = lax.optimization_barrier(
        (query_normed, value_parts[0], value_parts[2])
    )
    query_own = to_heads(query_normed)
    tiles = query_own.shape[0] // TILE
    key_parts = halo(key_own, hop)

    start = position // hop * tiles
    listed = lax.dynamic_slice_in_dim(kv_tiles, start, tiles, 0)
    own_frames = lax.dynamic_slice_in_dim(tile_frame, start, tiles, 0)
    gap = jnp.abs(own_frames[:, None] - jnp.take(tile_frame, listed, axis=0)).astype(jnp.float32)
    heads = narrow // HDIM
    own_slopes = lax.dynamic_slice_in_dim(slopes, member * heads, heads, 0)
    penalty = (own_slopes * LOG2E)[:, None] * gap.reshape(1, -1)
    index = (listed - (start - REACH)).reshape(-1)
    attended = attend(query_own, key_parts, value_parts, index, penalty.reshape(-1))
    attended = lax.all_to_all(
        attended.reshape(hop, groups * length, narrow),
        "blk",
        split_axis=0,
        concat_axis=0,
        axis_index_groups=lines,
        tiled=True,
    )
    attended = attended.transpose(1, 0, 2).reshape(groups * length, hop * narrow)

    rows = attended.shape[0] // groups
    width = full_columns.shape[1] // CHUNKS

    def partial(owner, chunk):
        return jnp.dot(
            lax.dynamic_slice_in_dim(attended, owner * rows, rows, 0),
            full_columns[:, chunk * width : (chunk + 1) * width],
            preferred_element_type=jnp.float32,
        ).astype(jnp.bfloat16)

    arrived = []
    for chunk in range(CHUNKS):
        arrived.append(
            [
                lax.ppermute(
                    partial(lax.rem(group + step, groups), chunk),
                    "head",
                    [(source, (source + step) % groups) for source in range(groups)],
                )
                for step in range(1, groups)
            ]
        )
    mixed = []
    for chunk in range(CHUNKS):
        floats = partial(group, chunk).astype(jnp.float32)
        for term in arrived[chunk]:
            floats = floats + term.astype(jnp.float32)
        mixed.append(floats.astype(jnp.bfloat16))
    return jnp.concatenate(mixed, axis=1)[None]


def shards(*arrays):
    queries, out_weight = arrays[0], arrays[6]
    rows = queries.shape[1]
    if lax.axis_size("head") == 2 and lax.axis_size("blk") % LINE == 0 and rows == TILE:
        if 2 * out_weight.shape[1] % HDIM == 0:
            return fused_shards(*arrays)
    return general_shards(*arrays)


def solution(mesh):
    placed = (
        P("head", "blk", None),
        P("head", "blk", None),
        P("head", "blk", None),
        P(),
        P(),
        P("head"),
        P("head", "blk"),
        P(),
        P(),
    )
    return jax.shard_map(
        shards, mesh=mesh, in_specs=placed, out_specs=P("head", "blk", None), check_vma=False
    )
```

```python
import math

import jax
import jax.numpy as jnp
from jax import lax
from jax.experimental import pallas as pl
from jax.experimental.pallas import tpu as pltpu
from jax.sharding import PartitionSpec as P

HDIM = 128
TILE = 384
REACH = 3
LOG2E = math.log2(math.e)
CHUNKS = 4
TEAM = 8
STEP = 2
LINE = 4
PIECES = 4
NORM_ROWS = 64
NORM_GROUP = 16
MESH = pl.DeviceIdType.MESH
FLIPS = ((1, 0, 0), (0, 1, 0), (1, 0, 1), (0, 1, 1), (1, 1, 0), (1, 1, 1), (0, 0, 1))
VMEM_LIMIT = 60 * 1024 * 1024


def fused_kernel(sizes, near_ref, frame_ref, slope_ref, q_gain_ref, k_gain_ref, q_ref, k_ref, v_ref, w_ref, out_ref, *scratch):
    planes, hpd, length, pair = sizes
    wins = REACH + 1
    slabs = TEAM * hpd
    per_tile = pair // HDIM
    narrow, inner = w_ref.shape
    key_wins, value_wins = scratch[:hpd], scratch[hpd : 2 * hpd]
    (queries, keys_n, queries_n, gathered, weight, arrived, raw) = scratch[2 * hpd : 2 * hpd + 7]
    (
        raw_sem,
        qkv_send,
        qkv_recv,
        qkv_local,
        halo_send,
        halo_recv,
        w_send,
        w_recv,
        w_local,
        att_send,
        att_recv,
        att_local,
        x_send,
        x_recv,
        y_send,
        y_recv,
        out_local,
    ) = scratch[2 * hpd + 7 :]

    x, b = lax.axis_index("head"), lax.axis_index("blk")
    z, m = b // LINE, b % LINE
    y, c = m // 2, m % 2
    me = m * 2 + x

    def device(xx, zz, mm):
        return (xx, zz * LINE + mm)

    def remote(src, dst, send, recv, target):
        copy = pltpu.make_async_remote_copy(
            src_ref=src, dst_ref=dst, send_sem=send, recv_sem=recv, device_id=target, device_id_type=MESH
        )
        copy.start()

    def local(src, dst, sem):
        pltpu.make_async_copy(src, dst, sem).start()

    def wait(like, sem):
        pltpu.make_async_copy(like, like, sem).wait()

    def lanes(at):
        return pl.ds(pl.multiple_of(at * HDIM, HDIM), HDIM)

    mates = []
    for dx, dy, dc in FLIPS:
        mates.append(((x + dx) % 2, ((y + dy) % 2) * 2 + (c + dc) % 2))
    planes_off = [(z + k) % planes for k in range(1, planes)]

    barrier = pltpu.get_barrier_semaphore()
    for xx, mm in mates:
        pl.semaphore_signal(barrier, inc=1, device_id=device(xx, z, mm), device_id_type=MESH)
    for zz in planes_off:
        pl.semaphore_signal(barrier, inc=1, device_id=device(x, zz, m), device_id_type=MESH)
    pl.semaphore_wait(barrier, len(mates) + len(planes_off))

    rail = pl.ds(pl.multiple_of(c * narrow, HDIM // 2), narrow)
    sibling = device(x, z, y * 2 + 1 - c)

    portion = narrow // PIECES

    def part_of(piece):
        return pl.ds(pl.multiple_of(c * narrow + piece * portion, 16), portion)

    def weight_along(block, source, step, piece):
        there = weight.at[block, part_of(piece)]
        arrival = w_recv.at[block * 2 + c, piece]
        if step >= 0:

            @pl.when(z < planes - 1)
            def _():
                remote(source, there, w_send.at[step, 0], arrival, device(x, z + 1, m))

        if step <= 0:

            @pl.when(z > 0)
            def _():
                remote(source, there, w_send.at[-step, 1], arrival, device(x, z - 1, m))

    def weight_across(block, source, step, piece):
        there = weight.at[block, part_of(piece)]
        remote(source, there, w_send.at[abs(step), 2 + (step < 0)], w_recv.at[block * 2 + c, piece], sibling)

    def weight_own(piece):
        weight_along(z, w_ref.at[pl.ds(piece * portion, portion)], 0, piece)

    def weight_forward(step, piece):
        for sign in (1, -1):

            @pl.when(z >= step if sign > 0 else z < planes - step)
            def _():
                block = z - sign * step
                here = weight.at[block, part_of(piece)]
                wait(here, w_recv.at[block * 2 + c, piece])
                weight_along(block, here, sign * step, piece)
                weight_across(block, here, sign * step, piece)

    def weight_left():
        @pl.when(z < planes - 1)
        def _():
            wait(w_ref, w_send.at[0, 0])

        @pl.when(z > 0)
        def _():
            wait(w_ref, w_send.at[0, 1])

        wait(w_ref, w_send.at[0, 2])
        for step in range(1, planes):
            for way in range(2):
                here = z >= step if way == 0 else z < planes - step
                onward = z < planes - 1 if way == 0 else z > 0

                @pl.when(here)
                def _():
                    wait(w_ref, w_send.at[step, 2 + way])

                @pl.when(here & onward)
                def _():
                    wait(w_ref, w_send.at[step, way])

    local(w_ref, weight.at[z, rail], w_local)
    for piece in range(PIECES):
        weight_across(z, w_ref.at[pl.ds(piece * portion, portion)], 0, piece)
    weight_own(0)
    weight_own(1)

    def scatter(kind, h, source, window, at, side=None):
        for (xx, mm), (dx, _, _) in zip(mates, FLIPS):
            if side is None or side == dx:
                head = (xx * LINE + mm) * hpd + h
                slot = kind + 1 if side == 0 else kind
                remote(source(head), window.at[at], qkv_send.at[slot], qkv_recv.at[slot, h], device(xx, z, mm))
        if side != 1:
            local(source((x * LINE + m) * hpd + h), window.at[at], qkv_local.at[kind, h])

    for h in range(hpd):
        scatter(0, h, lambda head: v_ref.at[0, :, lanes(head)], value_wins[h], REACH + me)

    def normed(source, gain_ref, scale, target):
        steps = length // NORM_ROWS

        def chunk(step, slot):
            return pltpu.make_async_copy(
                source.at[0, pl.ds(step * NORM_ROWS, NORM_ROWS)], raw.at[slot], raw_sem.at[slot]
            )

        chunk(0, 0).start()

        @pl.loop(0, steps)
        def _(step):
            slot = step % 2

            @pl.when(step + 1 < steps)
            def _():
                chunk(step + 1, 1 - slot).start()

            chunk(step, slot).wait()

            @pl.loop(0, NORM_ROWS // NORM_GROUP)
            def _(group):
                floats = raw[slot, pl.ds(group * NORM_GROUP, NORM_GROUP), :].astype(jnp.float32)
                factor = lax.rsqrt(jnp.mean(floats * floats, axis=-1, keepdims=True) + 1e-06)
                rows = (floats * (factor * scale) * gain_ref[...]).astype(jnp.bfloat16)
                at = pl.ds(step * NORM_ROWS + group * NORM_GROUP, NORM_GROUP)
                for slab in range(slabs):
                    target[slab, at, :] = rows[:, slab * HDIM : (slab + 1) * HDIM]

    normed(k_ref, k_gain_ref, 1.0, keys_n)
    normed(q_ref, q_gain_ref, LOG2E * HDIM ** (-0.5), queries_n)
    for h in range(hpd):
        scatter(1, h, lambda head: keys_n.at[head], key_wins[h], REACH + me)
        scatter(2, h, lambda head: queries_n.at[head], queries.at[h], me, 1)

    def landed(kind, h, window, first):
        wait(window.at[pl.ds(first, TEAM - 1)], qkv_recv.at[kind, h])
        wait(window.at[first], qkv_local.at[kind, h])

    top = REACH + TEAM

    def spread(kind, h, window):
        landed(kind, h, window, REACH)

        @pl.when(z < planes - 1)
        def _():
            remote(
                window.at[pl.ds(TEAM, REACH)],
                window.at[pl.ds(0, REACH)],
                halo_send.at[kind, 0, h],
                halo_recv.at[kind, 0, h],
                device(x, z + 1, m),
            )

        @pl.when(z > 0)
        def _():
            remote(
                window.at[pl.ds(REACH, REACH)],
                window.at[pl.ds(top, REACH)],
                halo_send.at[kind, 1, h],
                halo_recv.at[kind, 1, h],
                device(x, z - 1, m),
            )

    def halo_landed(h):
        for kind, window in ((0, value_wins[h]), (1, key_wins[h])):

            @pl.when(z > 0)
            def _():
                wait(window.at[pl.ds(0, REACH)], halo_recv.at[kind, 0, h])

            @pl.when(z < planes - 1)
            def _():
                wait(window.at[pl.ds(top, REACH)], halo_recv.at[kind, 1, h])

    def penalty(h, tile, near):
        gap = jnp.abs(frame_ref[tile] - frame_ref[near]).astype(jnp.float32)
        return slope_ref[m * hpd + h] * LOG2E * gap

    def attend(part, h):
        @pl.loop(0, LINE)
        def _(mm):
            tile = mm * 2 + (x + 1 - part) % 2
            at = z * TEAM + tile
            nears = [near_ref[win, at] for win in range(wins)]
            slots = [jnp.clip(near - (z * TEAM - REACH), 0, TEAM + 2 * REACH - 1) for near in nears]
            query = queries[h, tile]
            scores = []
            largest = None
            for win in range(wins):
                near = key_wins[h][slots[win]]
                score = lax.dot_general(
                    query, near, (((1,), (1,)), ((), ())), preferred_element_type=jnp.float32
                )
                less = penalty(h, at, nears[win])
                most = jnp.max(score, axis=-1, keepdims=True) - less
                largest = most if largest is None else jnp.maximum(largest, most)
                scores.append((score, less))
            total = jnp.zeros((length, 1), jnp.float32)
            summed = jnp.zeros((length, HDIM), jnp.float32)
            for win, (score, less) in enumerate(scores):
                share = jnp.exp2(score - (largest + less))
                total += jnp.sum(share, axis=-1, keepdims=True)
                summed += jnp.dot(
                    share.astype(jnp.bfloat16),
                    value_wins[h][slots[win]],
                    preferred_element_type=jnp.float32,
                )
            queries[h, tile] = (summed / total).astype(jnp.bfloat16)
            there = gathered.at[part * 2 + mm // 2, :, lanes(m * hpd + h)]
            core = mm % 2
            remote(
                queries.at[h, tile], there, att_send.at[0], att_recv.at[part], device(x, z, (1 - y) * 2 + core)
            )

            @pl.when(core == c)
            def _():
                local(queries.at[h, tile], there, att_local.at[part])

            @pl.when(core != c)
            def _():
                remote(queries.at[h, tile], there, att_send.at[1], att_recv.at[part], sibling)

    for h in range(hpd):
        spread(0, h, value_wins[h])
    waiting = [lambda piece=piece: weight_own(piece) for piece in range(2, PIECES)]
    waiting += [lambda piece=piece: weight_forward(1, piece) for piece in range(PIECES)]
    waiting.pop(0)()
    for h in range(hpd):
        spread(1, h, key_wins[h])
        wait(queries.at[h, pl.ds(0, LINE)], qkv_recv.at[2, h])
        if waiting:
            waiting.pop(0)()
        if h > 0:
            halo_landed(h - 1)
            attend(0, h - 1)
    halo_landed(hpd - 1)
    attend(0, hpd - 1)
    for h in range(hpd):
        scatter(2, h, lambda head: queries_n.at[head], queries.at[h], me, 0)
    for step in waiting:
        step()
    for piece in range(PIECES // 2):
        weight_forward(2, piece)

    def attend_own(h):
        wait(queries.at[h, pl.ds(0, LINE - 1)], qkv_recv.at[3, h])
        wait(queries.at[h, 0], qkv_local.at[2, h])
        attend(1, h)

    wait(keys_n.at[pl.ds(0, (TEAM - 1) * hpd)], qkv_send.at[1])

    def near_plane(k):
        if k == 0:
            return z
        if planes == 4:
            low, high = z % 2, z // 2
            return (high + k // 2) % 2 * 2 + (low + k % 2) % 2
        return (z + k) % planes

    def project(part, zz, first, width):
        return lax.dot_general(
            gathered[part * 2 : part * 2 + 2].reshape(2 * length, inner),
            weight[zz, first : first + width, :],
            (((1,), (1,)), ((), ())),
            preferred_element_type=jnp.float32,
        )

    spans = [(first, min(2 * HDIM, pair - first)) for first in range(0, pair, 2 * HDIM)]

    def attended_landed(part):
        wait(keys_n.at[pl.ds(0, 2 * (LINE - 1) * hpd)], att_recv.at[part])
        wait(keys_n.at[pl.ds(0, 2 * hpd)], att_local.at[part])

    attended_landed(0)
    per_plane = 2 * per_tile
    turns = [k * hpd // planes for k in range(planes + 1)]
    for k in range(planes):
        zz = near_plane(k)
        if k == 0:
            wait(weight.at[zz, rail], w_local)
        if k == 1:
            for piece in range(PIECES // 2, PIECES):
                weight_forward(2, piece)
        if k >= 3:
            for piece in range(PIECES):
                weight_forward(k, piece)
        for piece in range(PIECES):
            wait(weight.at[zz, pl.ds(0, portion)], w_recv.at[zz * 2 + 1 - c, piece])
        for first, width in spans:
            product = project(0, zz, first, width).astype(jnp.bfloat16)
            for row in range(2):
                for at in range(width // HDIM):
                    slab = k * per_plane + row * per_tile + first // HDIM + at
                    keys_n[slab] = product[row * length : (row + 1) * length, at * HDIM : (at + 1) * HDIM]
        remote(
            keys_n.at[pl.ds(k * per_plane, per_plane)],
            arrived.at[k],
            x_send.at[k],
            x_recv.at[k],
            device(1 - x, z, m),
        )
        for h in range(turns[k], turns[k + 1]):
            attend_own(h)

    wait(queries_n.at[pl.ds(0, LINE * hpd)], qkv_send.at[2])
    wait(queries_n.at[pl.ds(0, (LINE - 1) * hpd)], qkv_send.at[3])
    attended_landed(1)
    for k in range(planes):
        zz = near_plane(k)
        wait(arrived.at[k], x_recv.at[k])
        for first, width in spans:
            product = project(1, zz, first, width)
            for row in range(2):
                for at in range(width // HDIM):
                    lane = first // HDIM + at
                    slab = k * per_plane + row * per_tile + lane
                    floats = product[row * length : (row + 1) * length, at * HDIM : (at + 1) * HDIM]
                    floats = floats + arrived[k, row * per_tile + lane].astype(jnp.float32)
                    queries_n[slab] = floats.astype(jnp.bfloat16)

            @pl.loop(0, 2)
            def _(row):
                for at in range(width // HDIM):
                    lane = first // HDIM + at
                    source = queries_n.at[k * per_plane + row * per_tile + lane]
                    there = out_ref.at[0, :, lanes((zz * 2 + y) * per_tile + lane)]

                    @pl.when(row == y)
                    def _():
                        local(source, there, out_local)

                    @pl.when(row != y)
                    def _():
                        remote(source, there, y_send, y_recv, device(x, z, (1 - y) * 2 + c))

    half = planes * per_tile
    wait(queries_n.at[pl.ds(0, half)], y_recv)
    wait(queries_n.at[pl.ds(0, half)], out_local)
    wait(queries_n.at[pl.ds(0, half)], y_send)
    for k in range(planes):
        wait(arrived.at[k], x_send.at[k])
    wait(keys_n.at[pl.ds(0, (TEAM - 1) * hpd)], qkv_send.at[0])
    wait(keys_n, att_send.at[0])
    wait(keys_n.at[pl.ds(0, LINE * hpd)], att_send.at[1])
    weight_left()
    for h in range(hpd):
        for kind, window in ((0, value_wins[h]), (1, key_wins[h])):

            @pl.when(z < planes - 1)
            def _():
                wait(window.at[pl.ds(0, REACH)], halo_send.at[kind, 0, h])

            @pl.when(z > 0)
            def _():
                wait(window.at[pl.ds(0, REACH)], halo_send.at[kind, 1, h])


def fused_shards(queries, keys, values, q_gain, k_gain, slopes, out_weight, kv_tiles, tile_frame):
    blocks = lax.axis_size("blk")
    planes = blocks // LINE
    length, features = values.shape[1:]
    hpd = features // (TEAM * HDIM)
    inner, narrow = out_weight.shape
    pair = 2 * narrow

    def body(*refs):
        fused_kernel((planes, hpd, length, pair), *refs)

    dma, half = pltpu.SemaphoreType.DMA, jnp.bfloat16
    slabs = TEAM * hpd
    anywhere = pl.BlockSpec(memory_space=pl.ANY)
    smem = pl.BlockSpec(memory_space=pltpu.SMEM)
    vmem = pl.BlockSpec(memory_space=pltpu.VMEM)
    window = pltpu.VMEM((TEAM + 2 * REACH, length, HDIM), half)
    rows = TEAM * length
    return pl.pallas_call(
        body,
        in_specs=[smem, smem, smem, vmem, vmem, anywhere, anywhere, anywhere, anywhere],
        out_specs=anywhere,
        out_shape=jax.ShapeDtypeStruct((1, length, narrow * blocks), half),
        scratch_shapes=[window] * (2 * hpd)
        + [
            pltpu.VMEM((hpd, TEAM, length, HDIM), half),
            pltpu.VMEM((slabs, length, HDIM), half),
            pltpu.VMEM((slabs, length, HDIM), half),
            pltpu.VMEM((4, length, inner), half),
            pltpu.VMEM((planes, pair, inner), half),
            pltpu.VMEM((planes, 2 * pair // HDIM, length, HDIM), half),
            pltpu.VMEM((2, NORM_ROWS, features), half),
            dma((2,)),
            dma((4,)),
            dma((4, hpd)),
            dma((3, hpd)),
            dma((2, 2, hpd)),
            dma((2, 2, hpd)),
            dma((planes, 4)),
            dma((2 * planes, PIECES)),
            dma,
            dma((2,)),
            dma((2,)),
            dma((2,)),
            dma((planes,)),
            dma((planes,)),
            dma,
            dma,
            dma,
        ],
        compiler_params=pltpu.CompilerParams(
            vmem_limit_bytes=VMEM_LIMIT, collective_id=0, has_side_effects=True
        ),
        cost_estimate=pl.CostEstimate(
            flops=4 * rows * (REACH + 1) * TILE * hpd * HDIM + 4 * length * inner * narrow * blocks,
            bytes_accessed=8 * length * features + 2 * inner * narrow,
            transcendentals=rows * (REACH + 1) * TILE * hpd,
        ),
    )(
        kv_tiles.T,
        tile_frame,
        slopes,
        q_gain[None],
        k_gain[None],
        queries,
        keys,
        values,
        out_weight.T,
    )


def shifted(value, axis, steps):
    count = lax.axis_size(axis)
    initial, last = (max(0, -steps), min(count, count - steps))
    return lax.ppermute(value, axis, [(source, source + steps) for source in range(initial, last)])


def rms_norm(rows, gain):
    floats = rows.astype(jnp.float32)
    factor = lax.rsqrt(jnp.mean(floats * floats, axis=-1, keepdims=True) + 1e-06)
    return (floats * factor * gain).astype(jnp.bfloat16)


def attend_kernel(tiles, wins, parts, index_ref, penalty_ref, *refs):
    q_ref = refs[0]
    key_refs = refs[1 : 1 + parts]
    value_refs = refs[1 + parts : 1 + 2 * parts]
    out_ref, key_window, value_window = refs[1 + 2 * parts :]
    head = pl.program_id(0)
    first = pl.program_id(1) * STEP

    @pl.when(first == 0)
    def _():
        for window, blocks in ((key_window, key_refs), (value_window, value_refs)):
            at = 0
            for block in blocks:
                for tile in range(block.shape[0] // TILE):
                    window[at] = block[tile * TILE : (tile + 1) * TILE, :]
                    at += 1

    for step in range(STEP):
        tile = first + step
        query = q_ref[step * TILE : (step + 1) * TILE, :]
        scores = []
        largest = None
        for win in range(wins):
            near = key_window[index_ref[tile * wins + win]]
            score = lax.dot_general(
                query, near, (((1,), (1,)), ((), ())), preferred_element_type=jnp.float32
            )
            penalty = penalty_ref[(head * tiles + tile) * wins + win]
            top = jnp.max(score, axis=-1, keepdims=True) - penalty
            largest = top if largest is None else jnp.maximum(largest, top)
            scores.append((score, penalty))
        total = jnp.zeros((TILE, 1), jnp.float32)
        summed = jnp.zeros((TILE, HDIM), jnp.float32)
        for win, (score, penalty) in enumerate(scores):
            weight = jnp.exp2(score - (largest + penalty))
            total += jnp.sum(weight, axis=-1, keepdims=True)
            summed += jnp.dot(
                weight.astype(jnp.bfloat16),
                value_window[index_ref[tile * wins + win]],
                preferred_element_type=jnp.float32,
            )
        out_ref[step * TILE : (step + 1) * TILE, :] = (summed / total).astype(out_ref.dtype)


def attend(query, key_parts, value_parts, index, penalty):
    rows, width = query.shape
    heads, tiles, wins = width // HDIM, rows // TILE, index.shape[0] * TILE // rows
    window = sum(part.shape[0] for part in key_parts) // TILE

    def column(array):
        return pl.BlockSpec((array.shape[0], HDIM), lambda h, t, *_: (0, h))

    stepped = pl.BlockSpec((STEP * TILE, HDIM), lambda h, t, *_: (t, h))

    def body(*refs):
        attend_kernel(tiles, wins, len(key_parts), *refs)

    operands = (query, *key_parts, *value_parts)
    return pl.pallas_call(
        body,
        grid_spec=pltpu.PrefetchScalarGridSpec(
            num_scalar_prefetch=2,
            grid=(heads, tiles // STEP),
            in_specs=[stepped, *(column(array) for array in operands[1:])],
            out_specs=stepped,
            scratch_shapes=[pltpu.VMEM((window, TILE, HDIM), jnp.bfloat16)] * 2,
        ),
        out_shape=jax.ShapeDtypeStruct(query.shape, jnp.bfloat16),
        compiler_params=pltpu.CompilerParams(vmem_limit_bytes=48 * 1024 * 1024),
        cost_estimate=pl.CostEstimate(
            flops=4 * rows * wins * TILE * width,
            bytes_accessed=2 * sum(array.size for array in operands) + 2 * query.size,
            transcendentals=rows * wins * TILE * heads,
        ),
    )(index, penalty, *operands)


def halo(own, hop):
    reach = REACH * TILE
    lower = shifted(own[own.shape[0] - reach :], "blk", hop)
    upper = shifted(own[:reach], "blk", -hop)
    return [lower, own, upper]


def general_shards(queries, keys, values, q_gain, k_gain, slopes, out_weight, kv_tiles, tile_frame):
    groups, blocks = lax.axis_size("head"), lax.axis_size("blk")
    position, group = lax.axis_index("blk"), lax.axis_index("head")
    hop = TEAM // groups
    member = lax.rem(position, hop)
    teams = [
        [head * blocks + first + inner for inner in range(hop) for head in range(groups)]
        for first in range(0, blocks, hop)
    ]
    lines = [list(range(first, first + hop)) for first in range(0, blocks, hop)]
    length, features = values.shape[1:]
    narrow = features // TEAM

    def to_heads(rows):
        parts = rows.reshape(length, groups, hop, narrow).transpose(2, 1, 0, 3)
        parts = lax.all_to_all(
            parts.reshape(TEAM, length, narrow),
            ("head", "blk"),
            split_axis=0,
            concat_axis=0,
            axis_index_groups=teams,
            tiled=True,
        )
        return parts.reshape(TEAM * length, narrow)

    full_columns = lax.all_gather(out_weight, "blk", axis=1, tiled=True)
    value_own = to_heads(values[0])
    key_own = to_heads(rms_norm(keys[0], k_gain))
    value_parts = halo(value_own, hop)
    query_normed = rms_norm(queries[0], q_gain * (LOG2E * HDIM ** (-0.5)))
    query_normed, value_parts[0], value_parts[2] = lax.optimization_barrier(
        (query_normed, value_parts[0], value_parts[2])
    )
    query_own = to_heads(query_normed)
    tiles = query_own.shape[0] // TILE
    key_parts = halo(key_own, hop)

    start = position // hop * tiles
    listed = lax.dynamic_slice_in_dim(kv_tiles, start, tiles, 0)
    own_frames = lax.dynamic_slice_in_dim(tile_frame, start, tiles, 0)
    gap = jnp.abs(own_frames[:, None] - jnp.take(tile_frame, listed, axis=0)).astype(jnp.float32)
    heads = narrow // HDIM
    own_slopes = lax.dynamic_slice_in_dim(slopes, member * heads, heads, 0)
    penalty = (own_slopes * LOG2E)[:, None] * gap.reshape(1, -1)
    index = (listed - (start - REACH)).reshape(-1)
    attended = attend(query_own, key_parts, value_parts, index, penalty.reshape(-1))
    attended = lax.all_to_all(
        attended.reshape(hop, groups * length, narrow),
        "blk",
        split_axis=0,
        concat_axis=0,
        axis_index_groups=lines,
        tiled=True,
    )
    attended = attended.transpose(1, 0, 2).reshape(groups * length, hop * narrow)

    rows = attended.shape[0] // groups
    width = full_columns.shape[1] // CHUNKS

    def partial(owner, chunk):
        return jnp.dot(
            lax.dynamic_slice_in_dim(attended, owner * rows, rows, 0),
            full_columns[:, chunk * width : (chunk + 1) * width],
            preferred_element_type=jnp.float32,
        ).astype(jnp.bfloat16)

    arrived = []
    for chunk in range(CHUNKS):
        arrived.append(
            [
                lax.ppermute(
                    partial(lax.rem(group + step, groups), chunk),
                    "head",
                    [(source, (source + step) % groups) for source in range(groups)],
                )
                for step in range(1, groups)
            ]
        )
    mixed = []
    for chunk in range(CHUNKS):
        floats = partial(group, chunk).astype(jnp.float32)
        for term in arrived[chunk]:
            floats = floats + term.astype(jnp.float32)
        mixed.append(floats.astype(jnp.bfloat16))
    return jnp.concatenate(mixed, axis=1)[None]


def shards(*arrays):
    queries, out_weight = arrays[0], arrays[6]
    rows = queries.shape[1]
    if lax.axis_size("head") == 2 and lax.axis_size("blk") % LINE == 0 and rows == TILE:
        if out_weight.shape[1] % (HDIM // 2) == 0:
            return fused_shards(*arrays)
    return general_shards(*arrays)


def solution(mesh):
    placed = (
        P("head", "blk", None),
        P("head", "blk", None),
        P("head", "blk", None),
        P(),
        P(),
        P("head"),
        P("head", "blk"),
        P(),
        P(),
    )
    return jax.shard_map(
        shards, mesh=mesh, in_specs=placed, out_specs=P("head", "blk", None), check_vma=False
    )
```

```python
import math

import jax
import jax.numpy as jnp
from jax import lax
from jax.experimental import pallas as pl
from jax.experimental.pallas import tpu as pltpu
from jax.sharding import PartitionSpec as P

HDIM = 128
TILE = 384
REACH = 3
LOG2E = math.log2(math.e)
CHUNKS = 4
TEAM = 8
STEP = 2
LINE = 4
PIECES = 4
NORM_ROWS = 64
NORM_GROUP = 16
MESH = pl.DeviceIdType.MESH
FLIPS = ((1, 0, 0), (0, 1, 0), (1, 0, 1), (0, 1, 1), (1, 1, 0), (1, 1, 1), (0, 0, 1))
VMEM_LIMIT = 55 * 1024 * 1024


def fused_kernel(sizes, near_ref, frame_ref, slope_ref, q_gain_ref, k_gain_ref, q_ref, k_ref, v_ref, w_ref, out_ref, *scratch):
    planes, hpd, length, pair = sizes
    wins = REACH + 1
    slabs = TEAM * hpd
    per_tile = pair // HDIM
    narrow, inner = w_ref.shape
    key_wins, value_wins = scratch[:hpd], scratch[hpd : 2 * hpd]
    (queries, keys_n, queries_n, gathered, weight, arrived, raw) = scratch[2 * hpd : 2 * hpd + 7]
    (
        raw_sem,
        qkv_send,
        qkv_recv,
        qkv_local,
        halo_send,
        halo_recv,
        w_send,
        w_recv,
        w_local,
        att_send,
        att_recv,
        att_local,
        x_send,
        x_recv,
        y_send,
        y_recv,
        out_local,
    ) = scratch[2 * hpd + 7 :]

    x, b = lax.axis_index("head"), lax.axis_index("blk")
    z, m = b // LINE, b % LINE
    y, c = m // 2, m % 2
    me = m * 2 + x

    def device(xx, zz, mm):
        return (xx, zz * LINE + mm)

    def remote(src, dst, send, recv, target):
        copy = pltpu.make_async_remote_copy(
            src_ref=src, dst_ref=dst, send_sem=send, recv_sem=recv, device_id=target, device_id_type=MESH
        )
        copy.start()

    def local(src, dst, sem):
        pltpu.make_async_copy(src, dst, sem).start()

    def wait(like, sem):
        pltpu.make_async_copy(like, like, sem).wait()

    def lanes(at):
        return pl.ds(pl.multiple_of(at * HDIM, HDIM), HDIM)

    mates = []
    for dx, dy, dc in FLIPS:
        mates.append(((x + dx) % 2, ((y + dy) % 2) * 2 + (c + dc) % 2))
    planes_off = [(z + k) % planes for k in range(1, planes)]

    barrier = pltpu.get_barrier_semaphore()
    for xx, mm in mates:
        pl.semaphore_signal(barrier, inc=1, device_id=device(xx, z, mm), device_id_type=MESH)
    for zz in planes_off:
        pl.semaphore_signal(barrier, inc=1, device_id=device(x, zz, m), device_id_type=MESH)
    pl.semaphore_wait(barrier, len(mates) + len(planes_off))

    rail = pl.ds(pl.multiple_of(c * narrow, HDIM // 2), narrow)
    sibling = device(x, z, y * 2 + 1 - c)

    portion = narrow // PIECES

    def part_of(piece):
        return pl.ds(pl.multiple_of(c * narrow + piece * portion, 16), portion)

    def weight_along(block, source, step, piece):
        there = weight.at[block, part_of(piece)]
        arrival = w_recv.at[block * 2 + c, piece]
        if step >= 0:

            @pl.when(z < planes - 1)
            def _():
                remote(source, there, w_send.at[step, 0], arrival, device(x, z + 1, m))

        if step <= 0:

            @pl.when(z > 0)
            def _():
                remote(source, there, w_send.at[-step, 1], arrival, device(x, z - 1, m))

    def weight_across(block, source, step, piece):
        there = weight.at[block, part_of(piece)]
        remote(source, there, w_send.at[abs(step), 2 + (step < 0)], w_recv.at[block * 2 + c, piece], sibling)

    def weight_own(piece):
        weight_along(z, w_ref.at[pl.ds(piece * portion, portion)], 0, piece)

    def weight_forward(step, piece):
        for sign in (1, -1):

            @pl.when(z >= step if sign > 0 else z < planes - step)
            def _():
                block = z - sign * step
                here = weight.at[block, part_of(piece)]
                wait(here, w_recv.at[block * 2 + c, piece])
                weight_along(block, here, sign * step, piece)
                weight_across(block, here, sign * step, piece)

    def weight_left():
        @pl.when(z < planes - 1)
        def _():
            wait(w_ref, w_send.at[0, 0])

        @pl.when(z > 0)
        def _():
            wait(w_ref, w_send.at[0, 1])

        wait(w_ref, w_send.at[0, 2])
        for step in range(1, planes):
            for way in range(2):
                here = z >= step if way == 0 else z < planes - step
                onward = z < planes - 1 if way == 0 else z > 0

                @pl.when(here)
                def _():
                    wait(w_ref, w_send.at[step, 2 + way])

                @pl.when(here & onward)
                def _():
                    wait(w_ref, w_send.at[step, way])

    local(w_ref, weight.at[z, rail], w_local)
    for piece in range(PIECES):
        weight_across(z, w_ref.at[pl.ds(piece * portion, portion)], 0, piece)
    weight_own(0)
    weight_own(1)

    def scatter(kind, h, source, window, at, side=None):
        for (xx, mm), (dx, _, _) in zip(mates, FLIPS):
            if side is None or side == dx:
                head = (xx * LINE + mm) * hpd + h
                slot = kind + 1 if side == 0 else kind
                remote(source(head), window.at[at], qkv_send.at[slot], qkv_recv.at[slot, h], device(xx, z, mm))
        if side != 1:
            local(source((x * LINE + m) * hpd + h), window.at[at], qkv_local.at[kind, h])

    for h in range(hpd):
        scatter(0, h, lambda head: v_ref.at[0, :, lanes(head)], value_wins[h], REACH + me)

    def normed(source, gain_ref, scale, target):
        steps = length // NORM_ROWS

        def chunk(step, slot):
            return pltpu.make_async_copy(
                source.at[0, pl.ds(step * NORM_ROWS, NORM_ROWS)], raw.at[slot], raw_sem.at[slot]
            )

        chunk(0, 0).start()

        @pl.loop(0, steps)
        def _(step):
            slot = step % 2

            @pl.when(step + 1 < steps)
            def _():
                chunk(step + 1, 1 - slot).start()

            chunk(step, slot).wait()

            @pl.loop(0, NORM_ROWS // NORM_GROUP)
            def _(group):
                floats = raw[slot, pl.ds(group * NORM_GROUP, NORM_GROUP), :].astype(jnp.float32)
                factor = lax.rsqrt(jnp.mean(floats * floats, axis=-1, keepdims=True) + 1e-06)
                rows = (floats * (factor * scale) * gain_ref[...]).astype(jnp.bfloat16)
                at = pl.ds(step * NORM_ROWS + group * NORM_GROUP, NORM_GROUP)
                for slab in range(slabs):
                    target[slab, at, :] = rows[:, slab * HDIM : (slab + 1) * HDIM]

    normed(k_ref, k_gain_ref, 1.0, keys_n)
    normed(q_ref, q_gain_ref, LOG2E * HDIM ** (-0.5), queries_n)
    for h in range(hpd):
        scatter(1, h, lambda head: keys_n.at[head], key_wins[h], REACH + me)
        scatter(2, h, lambda head: queries_n.at[head], queries.at[h], me, 1)

    def landed(kind, h, window, first):
        wait(window.at[pl.ds(first, TEAM - 1)], qkv_recv.at[kind, h])
        wait(window.at[first], qkv_local.at[kind, h])

    top = REACH + TEAM

    def spread(kind, h, window):
        landed(kind, h, window, REACH)

        @pl.when(z < planes - 1)
        def _():
            remote(
                window.at[pl.ds(TEAM, REACH)],
                window.at[pl.ds(0, REACH)],
                halo_send.at[kind, 0, h],
                halo_recv.at[kind, 0, h],
                device(x, z + 1, m),
            )

        @pl.when(z > 0)
        def _():
            remote(
                window.at[pl.ds(REACH, REACH)],
                window.at[pl.ds(top, REACH)],
                halo_send.at[kind, 1, h],
                halo_recv.at[kind, 1, h],
                device(x, z - 1, m),
            )

    def halo_landed(h):
        for kind, window in ((0, value_wins[h]), (1, key_wins[h])):

            @pl.when(z > 0)
            def _():
                wait(window.at[pl.ds(0, REACH)], halo_recv.at[kind, 0, h])

            @pl.when(z < planes - 1)
            def _():
                wait(window.at[pl.ds(top, REACH)], halo_recv.at[kind, 1, h])

    def penalty(h, tile, near):
        gap = jnp.abs(frame_ref[tile] - frame_ref[near]).astype(jnp.float32)
        return slope_ref[m * hpd + h] * LOG2E * gap

    def attend(part, h):
        @pl.loop(0, LINE)
        def _(mm):
            tile = mm * 2 + (x + 1 - part) % 2
            at = z * TEAM + tile
            nears = [near_ref[win, at] for win in range(wins)]
            slots = [jnp.clip(near - (z * TEAM - REACH), 0, TEAM + 2 * REACH - 1) for near in nears]
            query = queries[h, tile]
            scores = []
            largest = None
            for win in range(wins):
                near = key_wins[h][slots[win]]
                score = lax.dot_general(
                    query, near, (((1,), (1,)), ((), ())), preferred_element_type=jnp.float32
                )
                less = penalty(h, at, nears[win])
                most = jnp.max(score, axis=-1, keepdims=True) - less
                largest = most if largest is None else jnp.maximum(largest, most)
                scores.append((score, less))
            total = jnp.zeros((length, 1), jnp.float32)
            summed = jnp.zeros((length, HDIM), jnp.float32)
            for win, (score, less) in enumerate(scores):
                share = jnp.exp2(score - (largest + less))
                total += jnp.sum(share, axis=-1, keepdims=True)
                summed += jnp.dot(
                    share.astype(jnp.bfloat16),
                    value_wins[h][slots[win]],
                    preferred_element_type=jnp.float32,
                )
            queries[h, tile] = (summed / total).astype(jnp.bfloat16)
            there = gathered.at[part * 2 + mm // 2, :, lanes(m * hpd + h)]
            core = mm % 2
            remote(
                queries.at[h, tile], there, att_send.at[0], att_recv.at[part], device(x, z, (1 - y) * 2 + core)
            )

            @pl.when(core == c)
            def _():
                local(queries.at[h, tile], there, att_local.at[part])

            @pl.when(core != c)
            def _():
                remote(queries.at[h, tile], there, att_send.at[1], att_recv.at[part], sibling)

    for h in range(hpd):
        spread(0, h, value_wins[h])
    waiting = [lambda piece=piece: weight_own(piece) for piece in range(2, PIECES)]
    waiting += [lambda piece=piece: weight_forward(1, piece) for piece in range(PIECES)]
    waiting.pop(0)()
    for h in range(hpd):
        spread(1, h, key_wins[h])
        wait(queries.at[h, pl.ds(0, LINE)], qkv_recv.at[2, h])
        if waiting:
            waiting.pop(0)()
        if h > 0:
            halo_landed(h - 1)
            attend(0, h - 1)
    halo_landed(hpd - 1)
    attend(0, hpd - 1)
    for h in range(hpd):
        scatter(2, h, lambda head: queries_n.at[head], queries.at[h], me, 0)
    for step in waiting:
        step()
    for piece in range(PIECES // 2):
        weight_forward(2, piece)

    def attend_own(h):
        wait(queries.at[h, pl.ds(0, LINE - 1)], qkv_recv.at[3, h])
        wait(queries.at[h, 0], qkv_local.at[2, h])
        attend(1, h)

    wait(keys_n.at[pl.ds(0, (TEAM - 1) * hpd)], qkv_send.at[1])

    def near_plane(k):
        if k == 0:
            return z
        if planes == 4:
            low, high = z % 2, z // 2
            return (high + k // 2) % 2 * 2 + (low + k % 2) % 2
        return (z + k) % planes

    def project(part, zz, first, width):
        return lax.dot_general(
            gathered[part * 2 : part * 2 + 2].reshape(2 * length, inner),
            weight[zz, first : first + width, :],
            (((1,), (1,)), ((), ())),
            preferred_element_type=jnp.float32,
        )

    spans = [(first, min(2 * HDIM, pair - first)) for first in range(0, pair, 2 * HDIM)]

    def attended_landed(part):
        wait(keys_n.at[pl.ds(0, 2 * (LINE - 1) * hpd)], att_recv.at[part])
        wait(keys_n.at[pl.ds(0, 2 * hpd)], att_local.at[part])

    attended_landed(0)
    per_plane = 2 * per_tile
    turns = [k * hpd // planes for k in range(planes + 1)]
    for k in range(planes):
        zz = near_plane(k)
        if k == 0:
            wait(weight.at[zz, rail], w_local)
        if k == 1:
            for piece in range(PIECES // 2, PIECES):
                weight_forward(2, piece)
        if k >= 3:
            for piece in range(PIECES):
                weight_forward(k, piece)
        for piece in range(PIECES):
            wait(weight.at[zz, pl.ds(0, portion)], w_recv.at[zz * 2 + 1 - c, piece])
        for first, width in spans:
            product = project(0, zz, first, width).astype(jnp.bfloat16)
            for row in range(2):
                for at in range(width // HDIM):
                    slab = k * per_plane + row * per_tile + first // HDIM + at
                    keys_n[slab] = product[row * length : (row + 1) * length, at * HDIM : (at + 1) * HDIM]
        remote(
            keys_n.at[pl.ds(k * per_plane, per_plane)],
            arrived.at[k],
            x_send.at[k],
            x_recv.at[k],
            device(1 - x, z, m),
        )
        for h in range(turns[k], turns[k + 1]):
            attend_own(h)

    wait(queries_n.at[pl.ds(0, LINE * hpd)], qkv_send.at[2])
    wait(queries_n.at[pl.ds(0, (LINE - 1) * hpd)], qkv_send.at[3])
    attended_landed(1)
    for k in range(planes):
        zz = near_plane(k)
        wait(arrived.at[k], x_recv.at[k])
        for first, width in spans:
            product = project(1, zz, first, width)
            for row in range(2):
                for at in range(width // HDIM):
                    lane = first // HDIM + at
                    slab = k * per_plane + row * per_tile + lane
                    floats = product[row * length : (row + 1) * length, at * HDIM : (at + 1) * HDIM]
                    floats = floats + arrived[k, row * per_tile + lane].astype(jnp.float32)
                    queries_n[slab] = floats.astype(jnp.bfloat16)

            @pl.loop(0, 2)
            def _(row):
                for at in range(width // HDIM):
                    lane = first // HDIM + at
                    source = queries_n.at[k * per_plane + row * per_tile + lane]
                    there = out_ref.at[0, :, lanes((zz * 2 + y) * per_tile + lane)]

                    @pl.when(row == y)
                    def _():
                        local(source, there, out_local)

                    @pl.when(row != y)
                    def _():
                        remote(source, there, y_send, y_recv, device(x, z, (1 - y) * 2 + c))

    half = planes * per_tile
    wait(queries_n.at[pl.ds(0, half)], y_recv)
    wait(queries_n.at[pl.ds(0, half)], out_local)
    wait(queries_n.at[pl.ds(0, half)], y_send)
    for k in range(planes):
        wait(arrived.at[k], x_send.at[k])
    wait(keys_n.at[pl.ds(0, (TEAM - 1) * hpd)], qkv_send.at[0])
    wait(keys_n, att_send.at[0])
    wait(keys_n.at[pl.ds(0, LINE * hpd)], att_send.at[1])
    weight_left()
    for h in range(hpd):
        for kind, window in ((0, value_wins[h]), (1, key_wins[h])):

            @pl.when(z < planes - 1)
            def _():
                wait(window.at[pl.ds(0, REACH)], halo_send.at[kind, 0, h])

            @pl.when(z > 0)
            def _():
                wait(window.at[pl.ds(0, REACH)], halo_send.at[kind, 1, h])


def fused_shards(queries, keys, values, q_gain, k_gain, slopes, out_weight, kv_tiles, tile_frame):
    blocks = lax.axis_size("blk")
    planes = blocks // LINE
    length, features = values.shape[1:]
    hpd = features // (TEAM * HDIM)
    inner, narrow = out_weight.shape
    pair = 2 * narrow

    def body(*refs):
        fused_kernel((planes, hpd, length, pair), *refs)

    dma, half = pltpu.SemaphoreType.DMA, jnp.bfloat16
    slabs = TEAM * hpd
    anywhere = pl.BlockSpec(memory_space=pl.ANY)
    far = pl.BlockSpec(memory_space=pltpu.HBM)
    smem = pl.BlockSpec(memory_space=pltpu.SMEM)
    vmem = pl.BlockSpec(memory_space=pltpu.VMEM)
    window = pltpu.VMEM((TEAM + 2 * REACH, length, HDIM), half)
    rows = TEAM * length
    return pl.pallas_call(
        body,
        in_specs=[smem, smem, smem, vmem, vmem, far, far, far, far],
        out_specs=anywhere,
        out_shape=pltpu.VMEM((1, length, narrow * blocks), half),
        scratch_shapes=[window] * (2 * hpd)
        + [
            pltpu.VMEM((hpd, TEAM, length, HDIM), half),
            pltpu.VMEM((slabs, length, HDIM), half),
            pltpu.VMEM((slabs, length, HDIM), half),
            pltpu.VMEM((4, length, inner), half),
            pltpu.VMEM((planes, pair, inner), half),
            pltpu.VMEM((planes, 2 * pair // HDIM, length, HDIM), half),
            pltpu.VMEM((2, NORM_ROWS, features), half),
            dma((2,)),
            dma((4,)),
            dma((4, hpd)),
            dma((3, hpd)),
            dma((2, 2, hpd)),
            dma((2, 2, hpd)),
            dma((planes, 4)),
            dma((2 * planes, PIECES)),
            dma,
            dma((2,)),
            dma((2,)),
            dma((2,)),
            dma((planes,)),
            dma((planes,)),
            dma,
            dma,
            dma,
        ],
        compiler_params=pltpu.CompilerParams(
            vmem_limit_bytes=VMEM_LIMIT, collective_id=0, has_side_effects=True
        ),
        cost_estimate=pl.CostEstimate(
            flops=4 * rows * (REACH + 1) * TILE * hpd * HDIM + 4 * length * inner * narrow * blocks,
            bytes_accessed=8 * length * features + 2 * inner * narrow,
            transcendentals=rows * (REACH + 1) * TILE * hpd,
        ),
    )(
        kv_tiles.T,
        tile_frame,
        slopes,
        q_gain[None],
        k_gain[None],
        queries,
        keys,
        values,
        out_weight.T,
    )


def shifted(value, axis, steps):
    count = lax.axis_size(axis)
    initial, last = (max(0, -steps), min(count, count - steps))
    return lax.ppermute(value, axis, [(source, source + steps) for source in range(initial, last)])


def rms_norm(rows, gain):
    floats = rows.astype(jnp.float32)
    factor = lax.rsqrt(jnp.mean(floats * floats, axis=-1, keepdims=True) + 1e-06)
    return (floats * factor * gain).astype(jnp.bfloat16)


def attend_kernel(tiles, wins, parts, index_ref, penalty_ref, *refs):
    q_ref = refs[0]
    key_refs = refs[1 : 1 + parts]
    value_refs = refs[1 + parts : 1 + 2 * parts]
    out_ref, key_window, value_window = refs[1 + 2 * parts :]
    head = pl.program_id(0)
    first = pl.program_id(1) * STEP

    @pl.when(first == 0)
    def _():
        for window, blocks in ((key_window, key_refs), (value_window, value_refs)):
            at = 0
            for block in blocks:
                for tile in range(block.shape[0] // TILE):
                    window[at] = block[tile * TILE : (tile + 1) * TILE, :]
                    at += 1

    for step in range(STEP):
        tile = first + step
        query = q_ref[step * TILE : (step + 1) * TILE, :]
        scores = []
        largest = None
        for win in range(wins):
            near = key_window[index_ref[tile * wins + win]]
            score = lax.dot_general(
                query, near, (((1,), (1,)), ((), ())), preferred_element_type=jnp.float32
            )
            penalty = penalty_ref[(head * tiles + tile) * wins + win]
            top = jnp.max(score, axis=-1, keepdims=True) - penalty
            largest = top if largest is None else jnp.maximum(largest, top)
            scores.append((score, penalty))
        total = jnp.zeros((TILE, 1), jnp.float32)
        summed = jnp.zeros((TILE, HDIM), jnp.float32)
        for win, (score, penalty) in enumerate(scores):
            weight = jnp.exp2(score - (largest + penalty))
            total += jnp.sum(weight, axis=-1, keepdims=True)
            summed += jnp.dot(
                weight.astype(jnp.bfloat16),
                value_window[index_ref[tile * wins + win]],
                preferred_element_type=jnp.float32,
            )
        out_ref[step * TILE : (step + 1) * TILE, :] = (summed / total).astype(out_ref.dtype)


def attend(query, key_parts, value_parts, index, penalty):
    rows, width = query.shape
    heads, tiles, wins = width // HDIM, rows // TILE, index.shape[0] * TILE // rows
    window = sum(part.shape[0] for part in key_parts) // TILE

    def column(array):
        return pl.BlockSpec((array.shape[0], HDIM), lambda h, t, *_: (0, h))

    stepped = pl.BlockSpec((STEP * TILE, HDIM), lambda h, t, *_: (t, h))

    def body(*refs):
        attend_kernel(tiles, wins, len(key_parts), *refs)

    operands = (query, *key_parts, *value_parts)
    return pl.pallas_call(
        body,
        grid_spec=pltpu.PrefetchScalarGridSpec(
            num_scalar_prefetch=2,
            grid=(heads, tiles // STEP),
            in_specs=[stepped, *(column(array) for array in operands[1:])],
            out_specs=stepped,
            scratch_shapes=[pltpu.VMEM((window, TILE, HDIM), jnp.bfloat16)] * 2,
        ),
        out_shape=jax.ShapeDtypeStruct(query.shape, jnp.bfloat16),
        compiler_params=pltpu.CompilerParams(vmem_limit_bytes=48 * 1024 * 1024),
        cost_estimate=pl.CostEstimate(
            flops=4 * rows * wins * TILE * width,
            bytes_accessed=2 * sum(array.size for array in operands) + 2 * query.size,
            transcendentals=rows * wins * TILE * heads,
        ),
    )(index, penalty, *operands)


def halo(own, hop):
    reach = REACH * TILE
    lower = shifted(own[own.shape[0] - reach :], "blk", hop)
    upper = shifted(own[:reach], "blk", -hop)
    return [lower, own, upper]


def general_shards(queries, keys, values, q_gain, k_gain, slopes, out_weight, kv_tiles, tile_frame):
    groups, blocks = lax.axis_size("head"), lax.axis_size("blk")
    position, group = lax.axis_index("blk"), lax.axis_index("head")
    hop = TEAM // groups
    member = lax.rem(position, hop)
    teams = [
        [head * blocks + first + inner for inner in range(hop) for head in range(groups)]
        for first in range(0, blocks, hop)
    ]
    lines = [list(range(first, first + hop)) for first in range(0, blocks, hop)]
    length, features = values.shape[1:]
    narrow = features // TEAM

    def to_heads(rows):
        parts = rows.reshape(length, groups, hop, narrow).transpose(2, 1, 0, 3)
        parts = lax.all_to_all(
            parts.reshape(TEAM, length, narrow),
            ("head", "blk"),
            split_axis=0,
            concat_axis=0,
            axis_index_groups=teams,
            tiled=True,
        )
        return parts.reshape(TEAM * length, narrow)

    full_columns = lax.all_gather(out_weight, "blk", axis=1, tiled=True)
    value_own = to_heads(values[0])
    key_own = to_heads(rms_norm(keys[0], k_gain))
    value_parts = halo(value_own, hop)
    query_normed = rms_norm(queries[0], q_gain * (LOG2E * HDIM ** (-0.5)))
    query_normed, value_parts[0], value_parts[2] = lax.optimization_barrier(
        (query_normed, value_parts[0], value_parts[2])
    )
    query_own = to_heads(query_normed)
    tiles = query_own.shape[0] // TILE
    key_parts = halo(key_own, hop)

    start = position // hop * tiles
    listed = lax.dynamic_slice_in_dim(kv_tiles, start, tiles, 0)
    own_frames = lax.dynamic_slice_in_dim(tile_frame, start, tiles, 0)
    gap = jnp.abs(own_frames[:, None] - jnp.take(tile_frame, listed, axis=0)).astype(jnp.float32)
    heads = narrow // HDIM
    own_slopes = lax.dynamic_slice_in_dim(slopes, member * heads, heads, 0)
    penalty = (own_slopes * LOG2E)[:, None] * gap.reshape(1, -1)
    index = (listed - (start - REACH)).reshape(-1)
    attended = attend(query_own, key_parts, value_parts, index, penalty.reshape(-1))
    attended = lax.all_to_all(
        attended.reshape(hop, groups * length, narrow),
        "blk",
        split_axis=0,
        concat_axis=0,
        axis_index_groups=lines,
        tiled=True,
    )
    attended = attended.transpose(1, 0, 2).reshape(groups * length, hop * narrow)

    rows = attended.shape[0] // groups
    width = full_columns.shape[1] // CHUNKS

    def partial(owner, chunk):
        return jnp.dot(
            lax.dynamic_slice_in_dim(attended, owner * rows, rows, 0),
            full_columns[:, chunk * width : (chunk + 1) * width],
            preferred_element_type=jnp.float32,
        ).astype(jnp.bfloat16)

    arrived = []
    for chunk in range(CHUNKS):
        arrived.append(
            [
                lax.ppermute(
                    partial(lax.rem(group + step, groups), chunk),
                    "head",
                    [(source, (source + step) % groups) for source in range(groups)],
                )
                for step in range(1, groups)
            ]
        )
    mixed = []
    for chunk in range(CHUNKS):
        floats = partial(group, chunk).astype(jnp.float32)
        for term in arrived[chunk]:
            floats = floats + term.astype(jnp.float32)
        mixed.append(floats.astype(jnp.bfloat16))
    return jnp.concatenate(mixed, axis=1)[None]


def shards(*arrays):
    queries, out_weight = arrays[0], arrays[6]
    rows = queries.shape[1]
    if lax.axis_size("head") == 2 and lax.axis_size("blk") % LINE == 0 and rows == TILE:
        if out_weight.shape[1] % (HDIM // 2) == 0:
            return fused_shards(*arrays)
    return general_shards(*arrays)


def solution(mesh):
    placed = (
        P("head", "blk", None),
        P("head", "blk", None),
        P("head", "blk", None),
        P(),
        P(),
        P("head"),
        P("head", "blk"),
        P(),
        P(),
    )
    return jax.shard_map(
        shards, mesh=mesh, in_specs=placed, out_specs=P("head", "blk", None), check_vma=False
    )
```

```python
import math

import jax
import jax.numpy as jnp
from jax import lax
from jax.experimental import pallas as pl
from jax.experimental.pallas import tpu as pltpu
from jax.sharding import PartitionSpec as P

HDIM = 128
TILE = 384
REACH = 3
LOG2E = math.log2(math.e)
CHUNKS = 4
TEAM = 8
STEP = 2
LINE = 4
PIECES = 4
NORM_ROWS = 64
NORM_GROUP = 16
MESH = pl.DeviceIdType.MESH
FLIPS = ((0, 1, 0), (1, 1, 0), (0, 1, 1), (1, 1, 1), (1, 0, 0), (1, 0, 1), (0, 0, 1))
VMEM_LIMIT = 55 * 1024 * 1024


def fused_kernel(sizes, near_ref, frame_ref, slope_ref, q_gain_ref, k_gain_ref, q_ref, k_ref, v_ref, w_ref, out_ref, *scratch):
    planes, hpd, length, pair = sizes
    wins = REACH + 1
    slabs = TEAM * hpd
    per_tile = pair // HDIM
    narrow, inner = w_ref.shape
    key_wins, value_wins = scratch[:hpd], scratch[hpd : 2 * hpd]
    (queries, keys_n, queries_n, gathered, weight, arrived, raw) = scratch[2 * hpd : 2 * hpd + 7]
    (
        raw_sem,
        qkv_send,
        qkv_recv,
        qkv_local,
        halo_send,
        halo_recv,
        w_send,
        w_recv,
        w_local,
        att_send,
        att_recv,
        att_local,
        x_send,
        x_recv,
        y_send,
        y_recv,
        out_local,
    ) = scratch[2 * hpd + 7 :]

    x, b = lax.axis_index("head"), lax.axis_index("blk")
    z, m = b // LINE, b % LINE
    y, c = m // 2, m % 2
    me = m * 2 + x

    def device(xx, zz, mm):
        return (xx, zz * LINE + mm)

    def remote(src, dst, send, recv, target):
        copy = pltpu.make_async_remote_copy(
            src_ref=src, dst_ref=dst, send_sem=send, recv_sem=recv, device_id=target, device_id_type=MESH
        )
        copy.start()

    def local(src, dst, sem):
        pltpu.make_async_copy(src, dst, sem).start()

    def wait(like, sem):
        pltpu.make_async_copy(like, like, sem).wait()

    def lanes(at):
        return pl.ds(pl.multiple_of(at * HDIM, HDIM), HDIM)

    mates = []
    for dx, dy, dc in FLIPS:
        mates.append(((x + dx) % 2, ((y + dy) % 2) * 2 + (c + dc) % 2))
    planes_off = [(z + k) % planes for k in range(1, planes)]

    barrier = pltpu.get_barrier_semaphore()
    for xx, mm in mates:
        pl.semaphore_signal(barrier, inc=1, device_id=device(xx, z, mm), device_id_type=MESH)
    for zz in planes_off:
        pl.semaphore_signal(barrier, inc=1, device_id=device(x, zz, m), device_id_type=MESH)
    pl.semaphore_wait(barrier, len(mates) + len(planes_off))

    rail = pl.ds(pl.multiple_of(c * narrow, HDIM // 2), narrow)
    sibling = device(x, z, y * 2 + 1 - c)

    portion = narrow // PIECES

    def part_of(piece):
        return pl.ds(pl.multiple_of(c * narrow + piece * portion, 16), portion)

    def weight_along(block, source, step, piece):
        there = weight.at[block, part_of(piece)]
        arrival = w_recv.at[block * 2 + c, piece]
        if step >= 0:

            @pl.when(z < planes - 1)
            def _():
                remote(source, there, w_send.at[step, 0], arrival, device(x, z + 1, m))

        if step <= 0:

            @pl.when(z > 0)
            def _():
                remote(source, there, w_send.at[-step, 1], arrival, device(x, z - 1, m))

    def weight_across(block, source, step, piece):
        there = weight.at[block, part_of(piece)]
        remote(source, there, w_send.at[abs(step), 2 + (step < 0)], w_recv.at[block * 2 + c, piece], sibling)

    def weight_own(piece):
        weight_along(z, w_ref.at[pl.ds(piece * portion, portion)], 0, piece)

    def weight_forward(step, piece):
        for sign in (1, -1):

            @pl.when(z >= step if sign > 0 else z < planes - step)
            def _():
                block = z - sign * step
                here = weight.at[block, part_of(piece)]
                wait(here, w_recv.at[block * 2 + c, piece])
                weight_along(block, here, sign * step, piece)
                weight_across(block, here, sign * step, piece)

    def weight_left():
        @pl.when(z < planes - 1)
        def _():
            wait(w_ref, w_send.at[0, 0])

        @pl.when(z > 0)
        def _():
            wait(w_ref, w_send.at[0, 1])

        wait(w_ref, w_send.at[0, 2])
        for step in range(1, planes):
            for way in range(2):
                here = z >= step if way == 0 else z < planes - step
                onward = z < planes - 1 if way == 0 else z > 0

                @pl.when(here)
                def _():
                    wait(w_ref, w_send.at[step, 2 + way])

                @pl.when(here & onward)
                def _():
                    wait(w_ref, w_send.at[step, way])

    local(w_ref, weight.at[z, rail], w_local)
    for piece in range(PIECES):
        weight_across(z, w_ref.at[pl.ds(piece * portion, portion)], 0, piece)
    weight_own(0)
    weight_own(1)

    def scatter(kind, h, source, window, at, side=None):
        for (xx, mm), (dx, _, _) in zip(mates, FLIPS):
            if side is None or side == dx:
                head = (xx * LINE + mm) * hpd + h
                slot = kind + 1 if side == 0 else kind
                remote(source(head), window.at[at], qkv_send.at[slot], qkv_recv.at[slot, h], device(xx, z, mm))
        if side != 1:
            local(source((x * LINE + m) * hpd + h), window.at[at], qkv_local.at[kind, h])

    for h in range(hpd):
        scatter(0, h, lambda head: v_ref.at[0, :, lanes(head)], value_wins[h], REACH + me)

    def normed(source, gain_ref, scale, target):
        steps = length // NORM_ROWS

        def chunk(step, slot):
            return pltpu.make_async_copy(
                source.at[0, pl.ds(step * NORM_ROWS, NORM_ROWS)], raw.at[slot], raw_sem.at[slot]
            )

        chunk(0, 0).start()

        @pl.loop(0, steps)
        def _(step):
            slot = step % 2

            @pl.when(step + 1 < steps)
            def _():
                chunk(step + 1, 1 - slot).start()

            chunk(step, slot).wait()

            @pl.loop(0, NORM_ROWS // NORM_GROUP)
            def _(group):
                floats = raw[slot, pl.ds(group * NORM_GROUP, NORM_GROUP), :].astype(jnp.float32)
                factor = lax.rsqrt(jnp.mean(floats * floats, axis=-1, keepdims=True) + 1e-06)
                rows = (floats * (factor * scale) * gain_ref[...]).astype(jnp.bfloat16)
                at = pl.ds(step * NORM_ROWS + group * NORM_GROUP, NORM_GROUP)
                for slab in range(slabs):
                    target[slab, at, :] = rows[:, slab * HDIM : (slab + 1) * HDIM]

    normed(k_ref, k_gain_ref, 1.0, keys_n)
    normed(q_ref, q_gain_ref, LOG2E * HDIM ** (-0.5), queries_n)
    for h in range(hpd):
        scatter(1, h, lambda head: keys_n.at[head], key_wins[h], REACH + me)
        scatter(2, h, lambda head: queries_n.at[head], queries.at[h], me, 1)

    def landed(kind, h, window, first):
        wait(window.at[pl.ds(first, TEAM - 1)], qkv_recv.at[kind, h])
        wait(window.at[first], qkv_local.at[kind, h])

    top = REACH + TEAM

    def spread(kind, h, window):
        landed(kind, h, window, REACH)

        @pl.when(z < planes - 1)
        def _():
            remote(
                window.at[pl.ds(TEAM, REACH)],
                window.at[pl.ds(0, REACH)],
                halo_send.at[kind, 0, h],
                halo_recv.at[kind, 0, h],
                device(x, z + 1, m),
            )

        @pl.when(z > 0)
        def _():
            remote(
                window.at[pl.ds(REACH, REACH)],
                window.at[pl.ds(top, REACH)],
                halo_send.at[kind, 1, h],
                halo_recv.at[kind, 1, h],
                device(x, z - 1, m),
            )

    def halo_landed(h):
        for kind, window in ((0, value_wins[h]), (1, key_wins[h])):

            @pl.when(z > 0)
            def _():
                wait(window.at[pl.ds(0, REACH)], halo_recv.at[kind, 0, h])

            @pl.when(z < planes - 1)
            def _():
                wait(window.at[pl.ds(top, REACH)], halo_recv.at[kind, 1, h])

    def penalty(h, tile, near):
        gap = jnp.abs(frame_ref[tile] - frame_ref[near]).astype(jnp.float32)
        return slope_ref[m * hpd + h] * LOG2E * gap

    def attend(part, h):
        @pl.loop(0, LINE)
        def _(mm):
            tile = mm * 2 + (x + 1 - part) % 2
            at = z * TEAM + tile
            nears = [near_ref[win, at] for win in range(wins)]
            slots = [jnp.clip(near - (z * TEAM - REACH), 0, TEAM + 2 * REACH - 1) for near in nears]
            query = queries[h, tile]
            scores = []
            largest = None
            for win in range(wins):
                near = key_wins[h][slots[win]]
                score = lax.dot_general(
                    query, near, (((1,), (1,)), ((), ())), preferred_element_type=jnp.float32
                )
                less = penalty(h, at, nears[win])
                most = jnp.max(score, axis=-1, keepdims=True) - less
                largest = most if largest is None else jnp.maximum(largest, most)
                scores.append((score, less))
            total = jnp.zeros((length, 1), jnp.float32)
            summed = jnp.zeros((length, HDIM), jnp.float32)
            for win, (score, less) in enumerate(scores):
                share = jnp.exp2(score - (largest + less))
                total += jnp.sum(share, axis=-1, keepdims=True)
                summed += jnp.dot(
                    share.astype(jnp.bfloat16),
                    value_wins[h][slots[win]],
                    preferred_element_type=jnp.float32,
                )
            queries[h, tile] = (summed / total).astype(jnp.bfloat16)
            there = gathered.at[part * 2 + mm // 2, :, lanes(m * hpd + h)]
            core = mm % 2
            remote(
                queries.at[h, tile], there, att_send.at[0], att_recv.at[part], device(x, z, (1 - y) * 2 + core)
            )

            @pl.when(core == c)
            def _():
                local(queries.at[h, tile], there, att_local.at[part])

            @pl.when(core != c)
            def _():
                remote(queries.at[h, tile], there, att_send.at[1], att_recv.at[part], sibling)

    for h in range(hpd):
        spread(0, h, value_wins[h])
    waiting = [lambda piece=piece: weight_own(piece) for piece in range(2, PIECES)]
    waiting += [lambda piece=piece: weight_forward(1, piece) for piece in range(PIECES)]
    waiting.pop(0)()
    for h in range(hpd):
        spread(1, h, key_wins[h])
        wait(queries.at[h, pl.ds(0, LINE)], qkv_recv.at[2, h])
        if waiting:
            waiting.pop(0)()
        if h > 0:
            halo_landed(h - 1)
            attend(0, h - 1)
    halo_landed(hpd - 1)
    attend(0, hpd - 1)
    for h in range(hpd):
        scatter(2, h, lambda head: queries_n.at[head], queries.at[h], me, 0)
    for step in waiting:
        step()
    for piece in range(PIECES // 2):
        weight_forward(2, piece)

    def attend_own(h):
        wait(queries.at[h, pl.ds(0, LINE - 1)], qkv_recv.at[3, h])
        wait(queries.at[h, 0], qkv_local.at[2, h])
        attend(1, h)

    wait(keys_n.at[pl.ds(0, (TEAM - 1) * hpd)], qkv_send.at[1])

    def near_plane(k):
        if k == 0:
            return z
        if planes == 4:
            low, high = z % 2, z // 2
            return (high + k // 2) % 2 * 2 + (low + k % 2) % 2
        return (z + k) % planes

    def project(part, zz, first, width):
        return lax.dot_general(
            gathered[part * 2 : part * 2 + 2].reshape(2 * length, inner),
            weight[zz, first : first + width, :],
            (((1,), (1,)), ((), ())),
            preferred_element_type=jnp.float32,
        )

    spans = [(first, min(2 * HDIM, pair - first)) for first in range(0, pair, 2 * HDIM)]

    def attended_landed(part):
        wait(keys_n.at[pl.ds(0, 2 * (LINE - 1) * hpd)], att_recv.at[part])
        wait(keys_n.at[pl.ds(0, 2 * hpd)], att_local.at[part])

    attended_landed(0)
    per_plane = 2 * per_tile
    turns = [k * hpd // planes for k in range(planes + 1)]
    for k in range(planes):
        zz = near_plane(k)
        if k == 0:
            wait(weight.at[zz, rail], w_local)
        if k == 1:
            for piece in range(PIECES // 2, PIECES):
                weight_forward(2, piece)
        if k >= 3:
            for piece in range(PIECES):
                weight_forward(k, piece)
        for piece in range(PIECES):
            wait(weight.at[zz, pl.ds(0, portion)], w_recv.at[zz * 2 + 1 - c, piece])
        for first, width in spans:
            product = project(0, zz, first, width).astype(jnp.bfloat16)
            for row in range(2):
                for at in range(width // HDIM):
                    slab = k * per_plane + row * per_tile + first // HDIM + at
                    keys_n[slab] = product[row * length : (row + 1) * length, at * HDIM : (at + 1) * HDIM]
        remote(
            keys_n.at[pl.ds(k * per_plane, per_plane)],
            arrived.at[k],
            x_send.at[k],
            x_recv.at[k],
            device(1 - x, z, m),
        )
        for h in range(turns[k], turns[k + 1]):
            attend_own(h)

    wait(queries_n.at[pl.ds(0, LINE * hpd)], qkv_send.at[2])
    wait(queries_n.at[pl.ds(0, (LINE - 1) * hpd)], qkv_send.at[3])
    attended_landed(1)
    for k in range(planes):
        zz = near_plane(k)
        wait(arrived.at[k], x_recv.at[k])
        for first, width in spans:
            product = project(1, zz, first, width)
            for row in range(2):
                for at in range(width // HDIM):
                    lane = first // HDIM + at
                    slab = k * per_plane + row * per_tile + lane
                    floats = product[row * length : (row + 1) * length, at * HDIM : (at + 1) * HDIM]
                    floats = floats + arrived[k, row * per_tile + lane].astype(jnp.float32)
                    queries_n[slab] = floats.astype(jnp.bfloat16)

            @pl.loop(0, 2)
            def _(row):
                for at in range(width // HDIM):
                    lane = first // HDIM + at
                    source = queries_n.at[k * per_plane + row * per_tile + lane]
                    there = out_ref.at[0, :, lanes((zz * 2 + y) * per_tile + lane)]

                    @pl.when(row == y)
                    def _():
                        local(source, there, out_local)

                    @pl.when(row != y)
                    def _():
                        remote(source, there, y_send, y_recv, device(x, z, (1 - y) * 2 + c))

    half = planes * per_tile
    wait(queries_n.at[pl.ds(0, half)], y_recv)
    wait(queries_n.at[pl.ds(0, half)], out_local)
    wait(queries_n.at[pl.ds(0, half)], y_send)
    for k in range(planes):
        wait(arrived.at[k], x_send.at[k])
    wait(keys_n.at[pl.ds(0, (TEAM - 1) * hpd)], qkv_send.at[0])
    wait(keys_n, att_send.at[0])
    wait(keys_n.at[pl.ds(0, LINE * hpd)], att_send.at[1])
    weight_left()
    for h in range(hpd):
        for kind, window in ((0, value_wins[h]), (1, key_wins[h])):

            @pl.when(z < planes - 1)
            def _():
                wait(window.at[pl.ds(0, REACH)], halo_send.at[kind, 0, h])

            @pl.when(z > 0)
            def _():
                wait(window.at[pl.ds(0, REACH)], halo_send.at[kind, 1, h])


def fused_shards(queries, keys, values, q_gain, k_gain, slopes, out_weight, kv_tiles, tile_frame):
    blocks = lax.axis_size("blk")
    planes = blocks // LINE
    length, features = values.shape[1:]
    hpd = features // (TEAM * HDIM)
    inner, narrow = out_weight.shape
    pair = 2 * narrow

    def body(*refs):
        fused_kernel((planes, hpd, length, pair), *refs)

    dma, half = pltpu.SemaphoreType.DMA, jnp.bfloat16
    slabs = TEAM * hpd
    anywhere = pl.BlockSpec(memory_space=pl.ANY)
    far = pl.BlockSpec(memory_space=pltpu.HBM)
    smem = pl.BlockSpec(memory_space=pltpu.SMEM)
    vmem = pl.BlockSpec(memory_space=pltpu.VMEM)
    window = pltpu.VMEM((TEAM + 2 * REACH, length, HDIM), half)
    rows = TEAM * length
    return pl.pallas_call(
        body,
        in_specs=[smem, smem, smem, vmem, vmem, far, far, far, far],
        out_specs=anywhere,
        out_shape=pltpu.VMEM((1, length, narrow * blocks), half),
        scratch_shapes=[window] * (2 * hpd)
        + [
            pltpu.VMEM((hpd, TEAM, length, HDIM), half),
            pltpu.VMEM((slabs, length, HDIM), half),
            pltpu.VMEM((slabs, length, HDIM), half),
            pltpu.VMEM((4, length, inner), half),
            pltpu.VMEM((planes, pair, inner), half),
            pltpu.VMEM((planes, 2 * pair // HDIM, length, HDIM), half),
            pltpu.VMEM((2, NORM_ROWS, features), half),
            dma((2,)),
            dma((4,)),
            dma((4, hpd)),
            dma((3, hpd)),
            dma((2, 2, hpd)),
            dma((2, 2, hpd)),
            dma((planes, 4)),
            dma((2 * planes, PIECES)),
            dma,
            dma((2,)),
            dma((2,)),
            dma((2,)),
            dma((planes,)),
            dma((planes,)),
            dma,
            dma,
            dma,
        ],
        compiler_params=pltpu.CompilerParams(
            vmem_limit_bytes=VMEM_LIMIT, collective_id=0, has_side_effects=True
        ),
        cost_estimate=pl.CostEstimate(
            flops=4 * rows * (REACH + 1) * TILE * hpd * HDIM + 4 * length * inner * narrow * blocks,
            bytes_accessed=8 * length * features + 2 * inner * narrow,
            transcendentals=rows * (REACH + 1) * TILE * hpd,
        ),
    )(
        kv_tiles.T,
        tile_frame,
        slopes,
        q_gain[None],
        k_gain[None],
        queries,
        keys,
        values,
        out_weight.T,
    )


def shifted(value, axis, steps):
    count = lax.axis_size(axis)
    initial, last = (max(0, -steps), min(count, count - steps))
    return lax.ppermute(value, axis, [(source, source + steps) for source in range(initial, last)])


def rms_norm(rows, gain):
    floats = rows.astype(jnp.float32)
    factor = lax.rsqrt(jnp.mean(floats * floats, axis=-1, keepdims=True) + 1e-06)
    return (floats * factor * gain).astype(jnp.bfloat16)


def attend_kernel(tiles, wins, parts, index_ref, penalty_ref, *refs):
    q_ref = refs[0]
    key_refs = refs[1 : 1 + parts]
    value_refs = refs[1 + parts : 1 + 2 * parts]
    out_ref, key_window, value_window = refs[1 + 2 * parts :]
    head = pl.program_id(0)
    first = pl.program_id(1) * STEP

    @pl.when(first == 0)
    def _():
        for window, blocks in ((key_window, key_refs), (value_window, value_refs)):
            at = 0
            for block in blocks:
                for tile in range(block.shape[0] // TILE):
                    window[at] = block[tile * TILE : (tile + 1) * TILE, :]
                    at += 1

    for step in range(STEP):
        tile = first + step
        query = q_ref[step * TILE : (step + 1) * TILE, :]
        scores = []
        largest = None
        for win in range(wins):
            near = key_window[index_ref[tile * wins + win]]
            score = lax.dot_general(
                query, near, (((1,), (1,)), ((), ())), preferred_element_type=jnp.float32
            )
            penalty = penalty_ref[(head * tiles + tile) * wins + win]
            top = jnp.max(score, axis=-1, keepdims=True) - penalty
            largest = top if largest is None else jnp.maximum(largest, top)
            scores.append((score, penalty))
        total = jnp.zeros((TILE, 1), jnp.float32)
        summed = jnp.zeros((TILE, HDIM), jnp.float32)
        for win, (score, penalty) in enumerate(scores):
            weight = jnp.exp2(score - (largest + penalty))
            total += jnp.sum(weight, axis=-1, keepdims=True)
            summed += jnp.dot(
                weight.astype(jnp.bfloat16),
                value_window[index_ref[tile * wins + win]],
                preferred_element_type=jnp.float32,
            )
        out_ref[step * TILE : (step + 1) * TILE, :] = (summed / total).astype(out_ref.dtype)


def attend(query, key_parts, value_parts, index, penalty):
    rows, width = query.shape
    heads, tiles, wins = width // HDIM, rows // TILE, index.shape[0] * TILE // rows
    window = sum(part.shape[0] for part in key_parts) // TILE

    def column(array):
        return pl.BlockSpec((array.shape[0], HDIM), lambda h, t, *_: (0, h))

    stepped = pl.BlockSpec((STEP * TILE, HDIM), lambda h, t, *_: (t, h))

    def body(*refs):
        attend_kernel(tiles, wins, len(key_parts), *refs)

    operands = (query, *key_parts, *value_parts)
    return pl.pallas_call(
        body,
        grid_spec=pltpu.PrefetchScalarGridSpec(
            num_scalar_prefetch=2,
            grid=(heads, tiles // STEP),
            in_specs=[stepped, *(column(array) for array in operands[1:])],
            out_specs=stepped,
            scratch_shapes=[pltpu.VMEM((window, TILE, HDIM), jnp.bfloat16)] * 2,
        ),
        out_shape=jax.ShapeDtypeStruct(query.shape, jnp.bfloat16),
        compiler_params=pltpu.CompilerParams(vmem_limit_bytes=48 * 1024 * 1024),
        cost_estimate=pl.CostEstimate(
            flops=4 * rows * wins * TILE * width,
            bytes_accessed=2 * sum(array.size for array in operands) + 2 * query.size,
            transcendentals=rows * wins * TILE * heads,
        ),
    )(index, penalty, *operands)


def halo(own, hop):
    reach = REACH * TILE
    lower = shifted(own[own.shape[0] - reach :], "blk", hop)
    upper = shifted(own[:reach], "blk", -hop)
    return [lower, own, upper]


def general_shards(queries, keys, values, q_gain, k_gain, slopes, out_weight, kv_tiles, tile_frame):
    groups, blocks = lax.axis_size("head"), lax.axis_size("blk")
    position, group = lax.axis_index("blk"), lax.axis_index("head")
    hop = TEAM // groups
    member = lax.rem(position, hop)
    teams = [
        [head * blocks + first + inner for inner in range(hop) for head in range(groups)]
        for first in range(0, blocks, hop)
    ]
    lines = [list(range(first, first + hop)) for first in range(0, blocks, hop)]
    length, features = values.shape[1:]
    narrow = features // TEAM

    def to_heads(rows):
        parts = rows.reshape(length, groups, hop, narrow).transpose(2, 1, 0, 3)
        parts = lax.all_to_all(
            parts.reshape(TEAM, length, narrow),
            ("head", "blk"),
            split_axis=0,
            concat_axis=0,
            axis_index_groups=teams,
            tiled=True,
        )
        return parts.reshape(TEAM * length, narrow)

    full_columns = lax.all_gather(out_weight, "blk", axis=1, tiled=True)
    value_own = to_heads(values[0])
    key_own = to_heads(rms_norm(keys[0], k_gain))
    value_parts = halo(value_own, hop)
    query_normed = rms_norm(queries[0], q_gain * (LOG2E * HDIM ** (-0.5)))
    query_normed, value_parts[0], value_parts[2] = lax.optimization_barrier(
        (query_normed, value_parts[0], value_parts[2])
    )
    query_own = to_heads(query_normed)
    tiles = query_own.shape[0] // TILE
    key_parts = halo(key_own, hop)

    start = position // hop * tiles
    listed = lax.dynamic_slice_in_dim(kv_tiles, start, tiles, 0)
    own_frames = lax.dynamic_slice_in_dim(tile_frame, start, tiles, 0)
    gap = jnp.abs(own_frames[:, None] - jnp.take(tile_frame, listed, axis=0)).astype(jnp.float32)
    heads = narrow // HDIM
    own_slopes = lax.dynamic_slice_in_dim(slopes, member * heads, heads, 0)
    penalty = (own_slopes * LOG2E)[:, None] * gap.reshape(1, -1)
    index = (listed - (start - REACH)).reshape(-1)
    attended = attend(query_own, key_parts, value_parts, index, penalty.reshape(-1))
    attended = lax.all_to_all(
        attended.reshape(hop, groups * length, narrow),
        "blk",
        split_axis=0,
        concat_axis=0,
        axis_index_groups=lines,
        tiled=True,
    )
    attended = attended.transpose(1, 0, 2).reshape(groups * length, hop * narrow)

    rows = attended.shape[0] // groups
    width = full_columns.shape[1] // CHUNKS

    def partial(owner, chunk):
        return jnp.dot(
            lax.dynamic_slice_in_dim(attended, owner * rows, rows, 0),
            full_columns[:, chunk * width : (chunk + 1) * width],
            preferred_element_type=jnp.float32,
        ).astype(jnp.bfloat16)

    arrived = []
    for chunk in range(CHUNKS):
        arrived.append(
            [
                lax.ppermute(
                    partial(lax.rem(group + step, groups), chunk),
                    "head",
                    [(source, (source + step) % groups) for source in range(groups)],
                )
                for step in range(1, groups)
            ]
        )
    mixed = []
    for chunk in range(CHUNKS):
        floats = partial(group, chunk).astype(jnp.float32)
        for term in arrived[chunk]:
            floats = floats + term.astype(jnp.float32)
        mixed.append(floats.astype(jnp.bfloat16))
    return jnp.concatenate(mixed, axis=1)[None]


def shards(*arrays):
    queries, out_weight = arrays[0], arrays[6]
    rows = queries.shape[1]
    if lax.axis_size("head") == 2 and lax.axis_size("blk") % LINE == 0 and rows == TILE:
        if out_weight.shape[1] % (HDIM // 2) == 0:
            return fused_shards(*arrays)
    return general_shards(*arrays)


def solution(mesh):
    placed = (
        P("head", "blk", None),
        P("head", "blk", None),
        P("head", "blk", None),
        P(),
        P(),
        P("head"),
        P("head", "blk"),
        P(),
        P(),
    )
    return jax.shard_map(
        shards, mesh=mesh, in_specs=placed, out_specs=P("head", "blk", None), check_vma=False
    )
```

```python
import math

import jax
import jax.numpy as jnp
from jax import lax
from jax.experimental import pallas as pl
from jax.experimental.pallas import tpu as pltpu
from jax.sharding import PartitionSpec as P

HDIM = 128
TILE = 384
REACH = 3
LOG2E = math.log2(math.e)
CHUNKS = 4
TEAM = 8
STEP = 2
LINE = 4
PIECES = 4
NORM_ROWS = 64
NORM_GROUP = 16
MESH = pl.DeviceIdType.MESH
FLIPS = ((0, 1, 0), (1, 1, 0), (0, 1, 1), (1, 1, 1), (1, 0, 0), (1, 0, 1), (0, 0, 1))
VMEM_LIMIT = 55 * 1024 * 1024


def fused_kernel(sizes, near_ref, frame_ref, slope_ref, q_gain_ref, k_gain_ref, q_ref, k_ref, v_ref, w_ref, out_ref, *scratch):
    planes, hpd, length, pair = sizes
    wins = REACH + 1
    slabs = TEAM * hpd
    per_tile = pair // HDIM
    narrow, inner = w_ref.shape
    key_wins, value_wins = scratch[:hpd], scratch[hpd : 2 * hpd]
    (queries, keys_n, queries_n, gathered, weight, arrived, raw) = scratch[2 * hpd : 2 * hpd + 7]
    (
        raw_sem,
        qkv_send,
        qkv_recv,
        qkv_local,
        halo_send,
        halo_recv,
        w_send,
        w_recv,
        w_local,
        att_send,
        att_recv,
        att_local,
        x_send,
        x_recv,
        y_send,
        y_recv,
        out_local,
    ) = scratch[2 * hpd + 7 :]

    x, b = lax.axis_index("head"), lax.axis_index("blk")
    z, m = b // LINE, b % LINE
    y, c = m // 2, m % 2
    me = m * 2 + x

    def device(xx, zz, mm):
        return (xx, zz * LINE + mm)

    def remote(src, dst, send, recv, target):
        copy = pltpu.make_async_remote_copy(
            src_ref=src, dst_ref=dst, send_sem=send, recv_sem=recv, device_id=target, device_id_type=MESH
        )
        copy.start()

    def local(src, dst, sem):
        pltpu.make_async_copy(src, dst, sem).start()

    def wait(like, sem):
        pltpu.make_async_copy(like, like, sem).wait()

    def lanes(at):
        return pl.ds(pl.multiple_of(at * HDIM, HDIM), HDIM)

    mates = []
    for dx, dy, dc in FLIPS:
        mates.append(((x + dx) % 2, ((y + dy) % 2) * 2 + (c + dc) % 2))
    planes_off = [(z + k) % planes for k in range(1, planes)]

    barrier = pltpu.get_barrier_semaphore()
    for xx, mm in mates:
        pl.semaphore_signal(barrier, inc=1, device_id=device(xx, z, mm), device_id_type=MESH)
    for zz in planes_off:
        pl.semaphore_signal(barrier, inc=1, device_id=device(x, zz, m), device_id_type=MESH)
    pl.semaphore_wait(barrier, len(mates) + len(planes_off))

    rail = pl.ds(pl.multiple_of(c * narrow, HDIM // 2), narrow)
    sibling = device(x, z, y * 2 + 1 - c)

    portion = narrow // PIECES

    def part_of(piece):
        return pl.ds(pl.multiple_of(c * narrow + piece * portion, 16), portion)

    def weight_along(block, source, step, piece):
        there = weight.at[block, part_of(piece)]
        arrival = w_recv.at[block * 2 + c, piece]
        if step >= 0:

            @pl.when(z < planes - 1)
            def _():
                remote(source, there, w_send.at[step, 0], arrival, device(x, z + 1, m))

        if step <= 0:

            @pl.when(z > 0)
            def _():
                remote(source, there, w_send.at[-step, 1], arrival, device(x, z - 1, m))

    def weight_across(block, source, step, piece):
        there = weight.at[block, part_of(piece)]
        remote(source, there, w_send.at[abs(step), 2 + (step < 0)], w_recv.at[block * 2 + c, piece], sibling)

    def weight_own(piece):
        weight_along(z, w_ref.at[pl.ds(piece * portion, portion)], 0, piece)

    def weight_forward(step, piece):
        for sign in (1, -1):

            @pl.when(z >= step if sign > 0 else z < planes - step)
            def _():
                block = z - sign * step
                here = weight.at[block, part_of(piece)]
                wait(here, w_recv.at[block * 2 + c, piece])
                weight_along(block, here, sign * step, piece)
                weight_across(block, here, sign * step, piece)

    def weight_left():
        @pl.when(z < planes - 1)
        def _():
            wait(w_ref, w_send.at[0, 0])

        @pl.when(z > 0)
        def _():
            wait(w_ref, w_send.at[0, 1])

        wait(w_ref, w_send.at[0, 2])
        for step in range(1, planes):
            for way in range(2):
                here = z >= step if way == 0 else z < planes - step
                onward = z < planes - 1 if way == 0 else z > 0

                @pl.when(here)
                def _():
                    wait(w_ref, w_send.at[step, 2 + way])

                @pl.when(here & onward)
                def _():
                    wait(w_ref, w_send.at[step, way])

    def scatter(kind, h, source, window, at, side=None):
        for (xx, mm), (dx, _, _) in zip(mates, FLIPS):
            if side is None or side == dx:
                head = (xx * LINE + mm) * hpd + h
                slot = kind + 1 if side == 0 else kind
                remote(source(head), window.at[at], qkv_send.at[slot], qkv_recv.at[slot, h], device(xx, z, mm))
        if side != 1:
            local(source((x * LINE + m) * hpd + h), window.at[at], qkv_local.at[kind, h])

    for h in range(hpd):
        scatter(0, h, lambda head: v_ref.at[0, :, lanes(head)], value_wins[h], REACH + me)

    local(w_ref, weight.at[z, rail], w_local)
    for piece in range(PIECES):
        weight_across(z, w_ref.at[pl.ds(piece * portion, portion)], 0, piece)
    weight_own(0)
    weight_own(1)

    def normed(source, gain_ref, scale, target):
        steps = length // NORM_ROWS

        def chunk(step, slot):
            return pltpu.make_async_copy(
                source.at[0, pl.ds(step * NORM_ROWS, NORM_ROWS)], raw.at[slot], raw_sem.at[slot]
            )

        chunk(0, 0).start()

        @pl.loop(0, steps)
        def _(step):
            slot = step % 2

            @pl.when(step + 1 < steps)
            def _():
                chunk(step + 1, 1 - slot).start()

            chunk(step, slot).wait()

            @pl.loop(0, NORM_ROWS // NORM_GROUP)
            def _(group):
                floats = raw[slot, pl.ds(group * NORM_GROUP, NORM_GROUP), :].astype(jnp.float32)
                factor = lax.rsqrt(jnp.mean(floats * floats, axis=-1, keepdims=True) + 1e-06)
                rows = (floats * (factor * scale) * gain_ref[...]).astype(jnp.bfloat16)
                at = pl.ds(step * NORM_ROWS + group * NORM_GROUP, NORM_GROUP)
                for slab in range(slabs):
                    target[slab, at, :] = rows[:, slab * HDIM : (slab + 1) * HDIM]

    normed(k_ref, k_gain_ref, 1.0, keys_n)
    normed(q_ref, q_gain_ref, LOG2E * HDIM ** (-0.5), queries_n)
    for h in range(hpd):
        scatter(1, h, lambda head: keys_n.at[head], key_wins[h], REACH + me)
        scatter(2, h, lambda head: queries_n.at[head], queries.at[h], me, 1)

    def landed(kind, h, window, first):
        wait(window.at[pl.ds(first, TEAM - 1)], qkv_recv.at[kind, h])
        wait(window.at[first], qkv_local.at[kind, h])

    top = REACH + TEAM

    def spread(kind, h, window):
        landed(kind, h, window, REACH)

        @pl.when(z < planes - 1)
        def _():
            remote(
                window.at[pl.ds(TEAM, REACH)],
                window.at[pl.ds(0, REACH)],
                halo_send.at[kind, 0, h],
                halo_recv.at[kind, 0, h],
                device(x, z + 1, m),
            )

        @pl.when(z > 0)
        def _():
            remote(
                window.at[pl.ds(REACH, REACH)],
                window.at[pl.ds(top, REACH)],
                halo_send.at[kind, 1, h],
                halo_recv.at[kind, 1, h],
                device(x, z - 1, m),
            )

    def halo_landed(h):
        for kind, window in ((0, value_wins[h]), (1, key_wins[h])):

            @pl.when(z > 0)
            def _():
                wait(window.at[pl.ds(0, REACH)], halo_recv.at[kind, 0, h])

            @pl.when(z < planes - 1)
            def _():
                wait(window.at[pl.ds(top, REACH)], halo_recv.at[kind, 1, h])

    def penalty(h, tile, near):
        gap = jnp.abs(frame_ref[tile] - frame_ref[near]).astype(jnp.float32)
        return slope_ref[m * hpd + h] * LOG2E * gap

    def attend(part, h):
        @pl.loop(0, LINE)
        def _(mm):
            tile = mm * 2 + (x + 1 - part) % 2
            at = z * TEAM + tile
            nears = [near_ref[win, at] for win in range(wins)]
            slots = [jnp.clip(near - (z * TEAM - REACH), 0, TEAM + 2 * REACH - 1) for near in nears]
            query = queries[h, tile]
            scores = []
            largest = None
            for win in range(wins):
                near = key_wins[h][slots[win]]
                score = lax.dot_general(
                    query, near, (((1,), (1,)), ((), ())), preferred_element_type=jnp.float32
                )
                less = penalty(h, at, nears[win])
                most = jnp.max(score, axis=-1, keepdims=True) - less
                largest = most if largest is None else jnp.maximum(largest, most)
                scores.append((score, less))
            total = jnp.zeros((length, 1), jnp.float32)
            summed = jnp.zeros((length, HDIM), jnp.float32)
            for win, (score, less) in enumerate(scores):
                share = jnp.exp2(score - (largest + less))
                total += jnp.sum(share, axis=-1, keepdims=True)
                summed += jnp.dot(
                    share.astype(jnp.bfloat16),
                    value_wins[h][slots[win]],
                    preferred_element_type=jnp.float32,
                )
            queries[h, tile] = (summed / total).astype(jnp.bfloat16)
            there = gathered.at[part * 2 + mm // 2, :, lanes(m * hpd + h)]
            core = mm % 2
            remote(
                queries.at[h, tile], there, att_send.at[0], att_recv.at[part], device(x, z, (1 - y) * 2 + core)
            )

            @pl.when(core == c)
            def _():
                local(queries.at[h, tile], there, att_local.at[part])

            @pl.when(core != c)
            def _():
                remote(queries.at[h, tile], there, att_send.at[1], att_recv.at[part], sibling)

    for h in range(hpd):
        spread(0, h, value_wins[h])
    waiting = [lambda piece=piece: weight_own(piece) for piece in range(2, PIECES)]
    waiting += [lambda piece=piece: weight_forward(1, piece) for piece in range(PIECES)]
    waiting.pop(0)()
    for h in range(hpd):
        spread(1, h, key_wins[h])
        wait(queries.at[h, pl.ds(0, LINE)], qkv_recv.at[2, h])
        if waiting:
            waiting.pop(0)()
        if h > 0:
            halo_landed(h - 1)
            attend(0, h - 1)
    halo_landed(hpd - 1)
    attend(0, hpd - 1)
    for h in range(hpd):
        scatter(2, h, lambda head: queries_n.at[head], queries.at[h], me, 0)
    for step in waiting:
        step()
    for piece in range(PIECES // 2):
        weight_forward(2, piece)

    def attend_own(h):
        wait(queries.at[h, pl.ds(0, LINE - 1)], qkv_recv.at[3, h])
        wait(queries.at[h, 0], qkv_local.at[2, h])
        attend(1, h)

    wait(keys_n.at[pl.ds(0, (TEAM - 1) * hpd)], qkv_send.at[1])

    def near_plane(k):
        if k == 0:
            return z
        if planes == 4:
            low, high = z % 2, z // 2
            return (high + k // 2) % 2 * 2 + (low + k % 2) % 2
        return (z + k) % planes

    def project(part, zz, first, width):
        return lax.dot_general(
            gathered[part * 2 : part * 2 + 2].reshape(2 * length, inner),
            weight[zz, first : first + width, :],
            (((1,), (1,)), ((), ())),
            preferred_element_type=jnp.float32,
        )

    spans = [(first, min(2 * HDIM, pair - first)) for first in range(0, pair, 2 * HDIM)]

    def attended_landed(part):
        wait(keys_n.at[pl.ds(0, 2 * (LINE - 1) * hpd)], att_recv.at[part])
        wait(keys_n.at[pl.ds(0, 2 * hpd)], att_local.at[part])

    attended_landed(0)
    per_plane = 2 * per_tile
    turns = [k * hpd // planes for k in range(planes + 1)]
    for k in range(planes):
        zz = near_plane(k)
        if k == 0:
            wait(weight.at[zz, rail], w_local)
        if k == 1:
            for piece in range(PIECES // 2, PIECES):
                weight_forward(2, piece)
        if k >= 3:
            for piece in range(PIECES):
                weight_forward(k, piece)
        for piece in range(PIECES):
            wait(weight.at[zz, pl.ds(0, portion)], w_recv.at[zz * 2 + 1 - c, piece])
        for first, width in spans:
            product = project(0, zz, first, width).astype(jnp.bfloat16)
            for row in range(2):
                for at in range(width // HDIM):
                    slab = k * per_plane + row * per_tile + first // HDIM + at
                    keys_n[slab] = product[row * length : (row + 1) * length, at * HDIM : (at + 1) * HDIM]
        remote(
            keys_n.at[pl.ds(k * per_plane, per_plane)],
            arrived.at[k],
            x_send.at[k],
            x_recv.at[k],
            device(1 - x, z, m),
        )
        for h in range(turns[k], turns[k + 1]):
            attend_own(h)

    wait(queries_n.at[pl.ds(0, LINE * hpd)], qkv_send.at[2])
    wait(queries_n.at[pl.ds(0, (LINE - 1) * hpd)], qkv_send.at[3])
    attended_landed(1)
    for k in range(planes):
        zz = near_plane(k)
        wait(arrived.at[k], x_recv.at[k])
        for first, width in spans:
            product = project(1, zz, first, width)
            for row in range(2):
                for at in range(width // HDIM):
                    lane = first // HDIM + at
                    slab = k * per_plane + row * per_tile + lane
                    floats = product[row * length : (row + 1) * length, at * HDIM : (at + 1) * HDIM]
                    floats = floats + arrived[k, row * per_tile + lane].astype(jnp.float32)
                    queries_n[slab] = floats.astype(jnp.bfloat16)

            @pl.loop(0, 2)
            def _(row):
                for at in range(width // HDIM):
                    lane = first // HDIM + at
                    source = queries_n.at[k * per_plane + row * per_tile + lane]
                    there = out_ref.at[0, :, lanes((zz * 2 + y) * per_tile + lane)]

                    @pl.when(row == y)
                    def _():
                        local(source, there, out_local)

                    @pl.when(row != y)
                    def _():
                        remote(source, there, y_send, y_recv, device(x, z, (1 - y) * 2 + c))

    half = planes * per_tile
    wait(queries_n.at[pl.ds(0, half)], y_recv)
    wait(queries_n.at[pl.ds(0, half)], out_local)
    wait(queries_n.at[pl.ds(0, half)], y_send)
    for k in range(planes):
        wait(arrived.at[k], x_send.at[k])
    wait(keys_n.at[pl.ds(0, (TEAM - 1) * hpd)], qkv_send.at[0])
    wait(keys_n, att_send.at[0])
    wait(keys_n.at[pl.ds(0, LINE * hpd)], att_send.at[1])
    weight_left()
    for h in range(hpd):
        for kind, window in ((0, value_wins[h]), (1, key_wins[h])):

            @pl.when(z < planes - 1)
            def _():
                wait(window.at[pl.ds(0, REACH)], halo_send.at[kind, 0, h])

            @pl.when(z > 0)
            def _():
                wait(window.at[pl.ds(0, REACH)], halo_send.at[kind, 1, h])


def fused_shards(queries, keys, values, q_gain, k_gain, slopes, out_weight, kv_tiles, tile_frame):
    blocks = lax.axis_size("blk")
    planes = blocks // LINE
    length, features = values.shape[1:]
    hpd = features // (TEAM * HDIM)
    inner, narrow = out_weight.shape
    pair = 2 * narrow

    def body(*refs):
        fused_kernel((planes, hpd, length, pair), *refs)

    dma, half = pltpu.SemaphoreType.DMA, jnp.bfloat16
    slabs = TEAM * hpd
    anywhere = pl.BlockSpec(memory_space=pl.ANY)
    far = pl.BlockSpec(memory_space=pltpu.HBM)
    smem = pl.BlockSpec(memory_space=pltpu.SMEM)
    vmem = pl.BlockSpec(memory_space=pltpu.VMEM)
    window = pltpu.VMEM((TEAM + 2 * REACH, length, HDIM), half)
    rows = TEAM * length
    return pl.pallas_call(
        body,
        in_specs=[smem, smem, smem, vmem, vmem, far, far, far, far],
        out_specs=anywhere,
        out_shape=pltpu.VMEM((1, length, narrow * blocks), half),
        scratch_shapes=[window] * (2 * hpd)
        + [
            pltpu.VMEM((hpd, TEAM, length, HDIM), half),
            pltpu.VMEM((slabs, length, HDIM), half),
            pltpu.VMEM((slabs, length, HDIM), half),
            pltpu.VMEM((4, length, inner), half),
            pltpu.VMEM((planes, pair, inner), half),
            pltpu.VMEM((planes, 2 * pair // HDIM, length, HDIM), half),
            pltpu.VMEM((2, NORM_ROWS, features), half),
            dma((2,)),
            dma((4,)),
            dma((4, hpd)),
            dma((3, hpd)),
            dma((2, 2, hpd)),
            dma((2, 2, hpd)),
            dma((planes, 4)),
            dma((2 * planes, PIECES)),
            dma,
            dma((2,)),
            dma((2,)),
            dma((2,)),
            dma((planes,)),
            dma((planes,)),
            dma,
            dma,
            dma,
        ],
        compiler_params=pltpu.CompilerParams(
            vmem_limit_bytes=VMEM_LIMIT, collective_id=0, has_side_effects=True
        ),
        cost_estimate=pl.CostEstimate(
            flops=4 * rows * (REACH + 1) * TILE * hpd * HDIM + 4 * length * inner * narrow * blocks,
            bytes_accessed=8 * length * features + 2 * inner * narrow,
            transcendentals=rows * (REACH + 1) * TILE * hpd,
        ),
    )(
        kv_tiles.T,
        tile_frame,
        slopes,
        q_gain[None],
        k_gain[None],
        queries,
        keys,
        values,
        out_weight.T,
    )


def shifted(value, axis, steps):
    count = lax.axis_size(axis)
    initial, last = (max(0, -steps), min(count, count - steps))
    return lax.ppermute(value, axis, [(source, source + steps) for source in range(initial, last)])


def rms_norm(rows, gain):
    floats = rows.astype(jnp.float32)
    factor = lax.rsqrt(jnp.mean(floats * floats, axis=-1, keepdims=True) + 1e-06)
    return (floats * factor * gain).astype(jnp.bfloat16)


def attend_kernel(tiles, wins, parts, index_ref, penalty_ref, *refs):
    q_ref = refs[0]
    key_refs = refs[1 : 1 + parts]
    value_refs = refs[1 + parts : 1 + 2 * parts]
    out_ref, key_window, value_window = refs[1 + 2 * parts :]
    head = pl.program_id(0)
    first = pl.program_id(1) * STEP

    @pl.when(first == 0)
    def _():
        for window, blocks in ((key_window, key_refs), (value_window, value_refs)):
            at = 0
            for block in blocks:
                for tile in range(block.shape[0] // TILE):
                    window[at] = block[tile * TILE : (tile + 1) * TILE, :]
                    at += 1

    for step in range(STEP):
        tile = first + step
        query = q_ref[step * TILE : (step + 1) * TILE, :]
        scores = []
        largest = None
        for win in range(wins):
            near = key_window[index_ref[tile * wins + win]]
            score = lax.dot_general(
                query, near, (((1,), (1,)), ((), ())), preferred_element_type=jnp.float32
            )
            penalty = penalty_ref[(head * tiles + tile) * wins + win]
            top = jnp.max(score, axis=-1, keepdims=True) - penalty
            largest = top if largest is None else jnp.maximum(largest, top)
            scores.append((score, penalty))
        total = jnp.zeros((TILE, 1), jnp.float32)
        summed = jnp.zeros((TILE, HDIM), jnp.float32)
        for win, (score, penalty) in enumerate(scores):
            weight = jnp.exp2(score - (largest + penalty))
            total += jnp.sum(weight, axis=-1, keepdims=True)
            summed += jnp.dot(
                weight.astype(jnp.bfloat16),
                value_window[index_ref[tile * wins + win]],
                preferred_element_type=jnp.float32,
            )
        out_ref[step * TILE : (step + 1) * TILE, :] = (summed / total).astype(out_ref.dtype)


def attend(query, key_parts, value_parts, index, penalty):
    rows, width = query.shape
    heads, tiles, wins = width // HDIM, rows // TILE, index.shape[0] * TILE // rows
    window = sum(part.shape[0] for part in key_parts) // TILE

    def column(array):
        return pl.BlockSpec((array.shape[0], HDIM), lambda h, t, *_: (0, h))

    stepped = pl.BlockSpec((STEP * TILE, HDIM), lambda h, t, *_: (t, h))

    def body(*refs):
        attend_kernel(tiles, wins, len(key_parts), *refs)

    operands = (query, *key_parts, *value_parts)
    return pl.pallas_call(
        body,
        grid_spec=pltpu.PrefetchScalarGridSpec(
            num_scalar_prefetch=2,
            grid=(heads, tiles // STEP),
            in_specs=[stepped, *(column(array) for array in operands[1:])],
            out_specs=stepped,
            scratch_shapes=[pltpu.VMEM((window, TILE, HDIM), jnp.bfloat16)] * 2,
        ),
        out_shape=jax.ShapeDtypeStruct(query.shape, jnp.bfloat16),
        compiler_params=pltpu.CompilerParams(vmem_limit_bytes=48 * 1024 * 1024),
        cost_estimate=pl.CostEstimate(
            flops=4 * rows * wins * TILE * width,
            bytes_accessed=2 * sum(array.size for array in operands) + 2 * query.size,
            transcendentals=rows * wins * TILE * heads,
        ),
    )(index, penalty, *operands)


def halo(own, hop):
    reach = REACH * TILE
    lower = shifted(own[own.shape[0] - reach :], "blk", hop)
    upper = shifted(own[:reach], "blk", -hop)
    return [lower, own, upper]


def general_shards(queries, keys, values, q_gain, k_gain, slopes, out_weight, kv_tiles, tile_frame):
    groups, blocks = lax.axis_size("head"), lax.axis_size("blk")
    position, group = lax.axis_index("blk"), lax.axis_index("head")
    hop = TEAM // groups
    member = lax.rem(position, hop)
    teams = [
        [head * blocks + first + inner for inner in range(hop) for head in range(groups)]
        for first in range(0, blocks, hop)
    ]
    lines = [list(range(first, first + hop)) for first in range(0, blocks, hop)]
    length, features = values.shape[1:]
    narrow = features // TEAM

    def to_heads(rows):
        parts = rows.reshape(length, groups, hop, narrow).transpose(2, 1, 0, 3)
        parts = lax.all_to_all(
            parts.reshape(TEAM, length, narrow),
            ("head", "blk"),
            split_axis=0,
            concat_axis=0,
            axis_index_groups=teams,
            tiled=True,
        )
        return parts.reshape(TEAM * length, narrow)

    full_columns = lax.all_gather(out_weight, "blk", axis=1, tiled=True)
    value_own = to_heads(values[0])
    key_own = to_heads(rms_norm(keys[0], k_gain))
    value_parts = halo(value_own, hop)
    query_normed = rms_norm(queries[0], q_gain * (LOG2E * HDIM ** (-0.5)))
    query_normed, value_parts[0], value_parts[2] = lax.optimization_barrier(
        (query_normed, value_parts[0], value_parts[2])
    )
    query_own = to_heads(query_normed)
    tiles = query_own.shape[0] // TILE
    key_parts = halo(key_own, hop)

    start = position // hop * tiles
    listed = lax.dynamic_slice_in_dim(kv_tiles, start, tiles, 0)
    own_frames = lax.dynamic_slice_in_dim(tile_frame, start, tiles, 0)
    gap = jnp.abs(own_frames[:, None] - jnp.take(tile_frame, listed, axis=0)).astype(jnp.float32)
    heads = narrow // HDIM
    own_slopes = lax.dynamic_slice_in_dim(slopes, member * heads, heads, 0)
    penalty = (own_slopes * LOG2E)[:, None] * gap.reshape(1, -1)
    index = (listed - (start - REACH)).reshape(-1)
    attended = attend(query_own, key_parts, value_parts, index, penalty.reshape(-1))
    attended = lax.all_to_all(
        attended.reshape(hop, groups * length, narrow),
        "blk",
        split_axis=0,
        concat_axis=0,
        axis_index_groups=lines,
        tiled=True,
    )
    attended = attended.transpose(1, 0, 2).reshape(groups * length, hop * narrow)

    rows = attended.shape[0] // groups
    width = full_columns.shape[1] // CHUNKS

    def partial(owner, chunk):
        return jnp.dot(
            lax.dynamic_slice_in_dim(attended, owner * rows, rows, 0),
            full_columns[:, chunk * width : (chunk + 1) * width],
            preferred_element_type=jnp.float32,
        ).astype(jnp.bfloat16)

    arrived = []
    for chunk in range(CHUNKS):
        arrived.append(
            [
                lax.ppermute(
                    partial(lax.rem(group + step, groups), chunk),
                    "head",
                    [(source, (source + step) % groups) for source in range(groups)],
                )
                for step in range(1, groups)
            ]
        )
    mixed = []
    for chunk in range(CHUNKS):
        floats = partial(group, chunk).astype(jnp.float32)
        for term in arrived[chunk]:
            floats = floats + term.astype(jnp.float32)
        mixed.append(floats.astype(jnp.bfloat16))
    return jnp.concatenate(mixed, axis=1)[None]


def shards(*arrays):
    queries, out_weight = arrays[0], arrays[6]
    rows = queries.shape[1]
    if lax.axis_size("head") == 2 and lax.axis_size("blk") % LINE == 0 and rows == TILE:
        if out_weight.shape[1] % (HDIM // 2) == 0:
            return fused_shards(*arrays)
    return general_shards(*arrays)


def solution(mesh):
    placed = (
        P("head", "blk", None),
        P("head", "blk", None),
        P("head", "blk", None),
        P(),
        P(),
        P("head"),
        P("head", "blk"),
        P(),
        P(),
    )
    return jax.shard_map(
        shards, mesh=mesh, in_specs=placed, out_specs=P("head", "blk", None), check_vma=False
    )
```
